32 devices in a mesh: slab: 2 (over x), samp: 8 (over z, y), tgt: 2 (over core).
Axes of the slice: x: 2, y: 2, z: 4, core: 2. Of those that a mesh axis runs over, the one named last changes fastest.
Arguments:
- coverage: bfloat16 [2048, 1024], P('samp', ('slab', 'tgt')), parts along dimension 1, may hold values from 0.29882812 to 3
- neighbours: int32 [2048, 128], P('samp'), may hold values from 0 to 2047, as said below
- nbr_weight: bfloat16 [2048, 128], P('samp'), may hold values from 0.099609375 to 1
- ploidy: int32 [2048], P('samp'), may hold values from 1 to 2
- gc_bin: int32 [1024], P(('slab', 'tgt')), parts along dimension 0, may hold values from 0 to 7
Outputs:
- copy_number: float32 [2048, 1024], P('samp', ('slab', 'tgt')), parts along dimension 1
The draws below stay inside these ranges and needn't reach their ends.
There are 2 independent parts, one for each index of `slab`. The reference program is written for one: setup_inputs(seed, part) draws one part's arguments, and reference() takes and returns one part's arrays. A program takes and returns all parts, laid end to end along the dimension named above; an argument that names none is the same for every part. Nothing has to cross between parts.
Inputs may be any that keep to these rules, and one draw needn't show every extreme that they name: `neighbours`: row s lists 128 distinct samples other than s. The rows of the 256 samples of one index of samp name, from the samples of each index of samp, only those of one block of 128 samples (block b holds local samples b*128 to b*128 + 127 of that index).
All inputs are finite; a program needn't handle non-finite values.
Results may differ from the reference program's by a relative error of at most 0.00065.
The reference program's roundings to bfloat16 on the way (of `norm_cov`, `norm_sq` and `gate`) count: a program that leaves them out, or rounds other values in their place, can miss the bound.
Values may be sent and summed in bfloat16 or wider, within the bound.
No kernel may reach another device: no remote copies, remote signals or barrier semaphores. Data moves between devices by JAX's collectives and lax.ppermute only.
A program may use at most 64 MiB of HBM per device.

```python
import math
import jax
import jax.numpy as jnp
from jax import lax

SAMP_DEV = 256
TGT = 512
NEIGH = 128
RBLK = 128
NGC = 8
SAMPLES = 2048
N_SAMP = 8


def draw_neighbours(key, part):
    key = jax.random.fold_in(key, 11)
    key_blocks, key_scores = jax.random.split(key)
    total = SAMP_DEV * N_SAMP
    per_dev = SAMP_DEV // RBLK
    pool = N_SAMP * RBLK
    chosen = jax.random.randint(key_blocks, (N_SAMP, N_SAMP), 0, per_dev)
    rows = jnp.arange(total, dtype=jnp.int32)
    owner = rows // SAMP_DEV
    within = rows % SAMP_DEV
    scores = jax.random.randint(key_scores, (total, pool), 0, 2 ** 18) * pool + jnp.arange(pool, dtype=jnp.int32)[None, :]
    self_pos = owner * RBLK + within % RBLK
    self_in = chosen[owner, owner] == within // RBLK
    hit = self_in[:, None] & (jnp.arange(pool, dtype=jnp.int32)[None, :] == self_pos[:, None])
    scores = jnp.where(hit, -1, scores)
    _, places = lax.top_k(scores, NEIGH)
    source = places // RBLK
    inner = places % RBLK
    block = chosen[owner[:, None], source]
    return (source * SAMP_DEV + block * RBLK + inner).astype(jnp.int32)


def with_ends(result, own_key, least, largest):
    spot = [jax.random.randint(jax.random.fold_in(own_key, axis), (), 0, length) for axis, length in enumerate(result.shape)]
    widest = result.shape.index(max(result.shape))
    next_to = spot[:widest] + [(spot[widest] + 1) % result.shape[widest]] + spot[widest + 1:]
    return result.at[tuple(spot)].set(least).at[tuple(next_to)].set(largest)


def shard_levels(key, shape, cuts, smallest, largest):
    def one(position, blocks):
        steps = jax.random.uniform(jax.random.fold_in(jax.random.fold_in(key, 6), position), (blocks,), jnp.float32, smallest / len(cuts), largest / len(cuts))
        return jnp.repeat(jnp.exp(steps), shape[position] // blocks).reshape((-1,) + (1,) * (len(shape) - position - 1))

    loudness = one(*cuts[0])
    for cut in cuts[1:]:
        loudness = loudness * one(*cut)
    return loudness


def setup_inputs(seed: int = 0, part: int = 0) -> dict:
    key_list = jax.random.split(jax.random.key(seed), 6)
    part_keys = jax.random.split(jax.random.fold_in(key_list[5], part), 6)
    return {
        "coverage": jnp.clip(jnp.exp(math.log(3.0) - 2.306499 * jax.random.uniform(part_keys[0], (SAMPLES, TGT), jnp.float32) ** shard_levels(part_keys[0], (SAMPLES, TGT), ((0, 8), (1, 2)), -0.2, 0.2)), 0.29882812, 3.0).astype(jnp.bfloat16),
        "neighbours": draw_neighbours(jax.random.fold_in(key_list[5], 71), part),
        "nbr_weight": jnp.clip(jnp.exp(math.log(1.0) - 2.306499 * jax.random.uniform(key_list[2], (SAMPLES, NEIGH), jnp.float32) ** shard_levels(key_list[2], (SAMPLES, NEIGH), ((0, 8),), -0.2, 0.2)), 0.099609375, 1.0).astype(jnp.bfloat16),
        "ploidy": with_ends(jax.random.randint(key_list[3], (SAMPLES,), 1, 3), jax.random.fold_in(key_list[3], 1), 1, 2).astype(jnp.int32),
        "gc_bin": with_ends(jax.random.randint(part_keys[4], (TGT,), 0, NGC), jax.random.fold_in(part_keys[4], 1), 0, NGC - 1).astype(jnp.int32),
    }


LOG_PRIOR = (-4.6051702, -3.2188758, -0.1625189, -2.8134107, -3.5065579, -4.6051702)


def normalize_rows(covf, bin_sum, bin_count, onehot):
    sample_mean = jnp.sum(bin_sum, axis=1) / TGT
    bin_mean = bin_sum / jnp.maximum(bin_count, 1.0)[None, :]
    spread_mean = jnp.dot(bin_mean, onehot.T, precision=lax.Precision.HIGHEST)
    return (covf * (sample_mean[:, None] / spread_mean)).astype(jnp.bfloat16)


def spread_terms(first, second, third):
    ref_mean = second / first
    rel_var = (third / first - ref_mean * ref_mean) / (ref_mean * ref_mean)
    return ref_mean, rel_var


def copy_calls(normf, ref_mean, rel_var, rel_total, plf):
    level = 0.5 * rel_var + 0.5 * (rel_total / TGT)[:, None]
    ratio = normf / ref_mean
    scores = []
    for state in range(6):
        centre = max(state, 0.1) / plf
        vari = level * jnp.maximum(centre, 0.25) + 0.01
        delta = ratio - centre
        scores.append(LOG_PRIOR[state] - 0.5 * delta * delta / vari - 0.5 * jnp.log(vari))
    stacked = jnp.stack(scores)
    peak = jnp.max(stacked, axis=0)
    expo = jnp.exp(stacked - peak[None])
    states = jnp.arange(6, dtype=jnp.float32)[:, None, None]
    return jnp.sum(states * expo, axis=0) / jnp.sum(expo, axis=0)


def moments(table, neighbours, nbr_weight):
    count = neighbours.shape[0] // RBLK

    def one_block(args):
        index, weight = args
        picked = table[index].astype(jnp.float32)
        return jnp.einsum("sk,skt->st", weight.astype(jnp.float32), picked, precision=lax.Precision.HIGHEST)

    out = lax.map(one_block, (neighbours.reshape(count, RBLK, NEIGH), nbr_weight.reshape(count, RBLK, NEIGH)))
    return out.reshape(neighbours.shape[0], table.shape[1])


def reference(coverage, neighbours, nbr_weight, ploidy, gc_bin):
    covf = coverage.astype(jnp.float32)
    onehot = (gc_bin[:, None] == jnp.arange(NGC, dtype=jnp.int32)[None, :]).astype(jnp.float32)
    bin_sum = jnp.dot(covf, onehot, precision=lax.Precision.HIGHEST)
    bin_count = jnp.sum(onehot, axis=0)
    norm_cov = normalize_rows(covf, bin_sum, bin_count, onehot)
    normf = norm_cov.astype(jnp.float32)
    norm_sq = (normf * normf).astype(jnp.bfloat16)
    plf = ploidy.astype(jnp.float32)[:, None]
    first = jnp.sum(nbr_weight.astype(jnp.float32), axis=1)[:, None] * jnp.ones_like(normf)
    second = moments(norm_cov, neighbours, nbr_weight)
    third = moments(norm_sq, neighbours, nbr_weight)
    ref_mean, rel_var = spread_terms(first, second, third)
    first_call = copy_calls(normf, ref_mean, rel_var, jnp.sum(rel_var, axis=1), plf)
    offset = first_call - plf
    gate = (1.0 / (1.0 + 4.0 * offset * offset)).astype(jnp.bfloat16)
    gatef = gate.astype(jnp.float32)
    gated_cov = (gatef * normf).astype(jnp.bfloat16)
    gated_sq = (gatef * norm_sq.astype(jnp.float32)).astype(jnp.bfloat16)
    first = moments(gate, neighbours, nbr_weight)
    second = moments(gated_cov, neighbours, nbr_weight)
    third = moments(gated_sq, neighbours, nbr_weight)
    ref_mean, rel_var = spread_terms(first, second, third)
    return copy_calls(normf, ref_mean, rel_var, jnp.sum(rel_var, axis=1), plf)
```

```python
import jax
import jax.numpy as jnp
from jax import lax
from jax.sharding import PartitionSpec as P

TGT = 512
NGC = 8
RBLK = 128
EXTRA = 16


LOG_PRIOR = (-4.6051702, -3.2188758, -0.1625189, -2.8134107, -3.5065579, -4.6051702)


def swap_tgt(value):
    return lax.ppermute(value, "tgt", [(0, 1), (1, 0)])


def send(value, step, count):
    return lax.ppermute(value, "samp", [(i, i ^ step) for i in range(count)])


def pick(block, which):
    return lax.dynamic_slice_in_dim(block, which * RBLK, RBLK, axis=0)


def spread_terms(first, second, third):
    ref_mean = second / first
    rel_var = (third / first - ref_mean * ref_mean) / (ref_mean * ref_mean)
    return (ref_mean, rel_var)


def copy_calls(normf, ref_mean, rel_var, plf):
    part = jnp.sum(rel_var, axis=1)
    rel_total = part + swap_tgt(part)
    level = 0.5 * rel_var + 0.5 * (rel_total / TGT)[:, None]
    ratio = normf / ref_mean
    scores = []
    for state in range(6):
        centre = max(state, 0.1) / plf
        vari = level * jnp.maximum(centre, 0.25) + 0.01
        delta = ratio - centre
        scores.append(LOG_PRIOR[state] - 0.5 * delta * delta / vari - 0.5 * jnp.log(vari))
    peak = scores[0]
    for score in scores[1:]:
        peak = jnp.maximum(peak, score)
    expo = [jnp.exp(score - peak) for score in scores]
    top = sum(state * expo[state] for state in range(1, 6))
    return top / sum(expo)


def weighted(weight_map, table):
    return jnp.dot(weight_map, table, preferred_element_type=jnp.float32)


def squared(table):
    tablef = table.astype(jnp.float32)
    return (tablef * tablef).astype(jnp.bfloat16)


def build_map(position, low, nbr_weight, count):
    high_one = jnp.where(
        position[:, :, None] == jnp.arange(count, dtype=jnp.int32)[None, None, :],
        nbr_weight[:, :, None],
        jnp.zeros((), jnp.bfloat16),
    )
    low_one = (low[:, :, None] == jnp.arange(RBLK, dtype=jnp.int32)[None, None, :]).astype(
        jnp.bfloat16
    )
    table = jnp.einsum("skg,skl->sgl", high_one, low_one, preferred_element_type=jnp.float32)
    return table.astype(jnp.bfloat16).reshape(position.shape[0], count * RBLK)


def body(coverage, neighbours, nbr_weight, ploidy, gc_bin):
    count = lax.axis_size("samp")
    half = count // 2
    me = lax.axis_index("samp")
    rows, cols = coverage.shape
    covf = coverage.astype(jnp.float32)
    onehot = gc_bin[:, None] == jnp.arange(NGC, dtype=jnp.int32)[None, :]
    bin_sum = jnp.dot(coverage, onehot.astype(jnp.bfloat16), preferred_element_type=jnp.float32)
    onehot = onehot.astype(jnp.float32)
    stats = jnp.concatenate([bin_sum, jnp.sum(onehot, axis=0)[None, :]], axis=0)
    stats = stats + swap_tgt(stats)
    bin_sum, bin_count = stats[:rows], stats[rows]
    sample_mean = jnp.sum(bin_sum, axis=1) / TGT
    bin_mean = bin_sum / jnp.maximum(bin_count, 1.0)[None, :]
    spread_mean = jnp.dot(bin_mean, onehot.T, precision=lax.Precision.HIGHEST)
    norm_cov = (covf * (sample_mean[:, None] / spread_mean)).astype(jnp.bfloat16)
    normf = norm_cov.astype(jnp.float32)
    plf = ploidy.astype(jnp.float32)[:, None]

    position = (neighbours // rows) ^ me
    block = (neighbours // RBLK) % (rows // RBLK)
    low = neighbours % RBLK
    lanes = jnp.arange(count, dtype=jnp.int32)
    choice = jnp.max(
        jnp.where(position[:, :, None] == lanes[None, None, :], block[:, :, None], 0), axis=(0, 1)
    )
    note = jnp.zeros((EXTRA, cols), jnp.bfloat16).at[:, :count].set(
        jnp.broadcast_to(choice.astype(jnp.bfloat16)[None, :], (EXTRA, count))
    )

    noted = jnp.concatenate([norm_cov, note], axis=0)
    across = send(norm_cov, half, count)
    direct = {k: send(noted, k, count) for k in range(1, half)}
    wants = {
        k: (direct[k][rows, k].astype(jnp.int32), direct[k][rows, k ^ half].astype(jnp.int32))
        for k in direct
    }
    passed = {k: send(pick(across, wants[k][1]), k, count) for k in direct}
    near = [pick(norm_cov, choice[0])]
    near += [pick(direct[k], choice[k]) for k in direct]
    near += [pick(across, choice[half])]
    near += [passed[k] for k in direct]
    near_cov = jnp.concatenate(near, axis=0)
    near_sq = squared(near_cov)

    weight_map = build_map(position, low, nbr_weight, count)
    first = jnp.sum(nbr_weight.astype(jnp.float32), axis=1)[:, None] * jnp.ones_like(normf)
    ref_mean, rel_var = spread_terms(
        first, weighted(weight_map, near_cov), weighted(weight_map, near_sq)
    )
    first_call = copy_calls(normf, ref_mean, rel_var, plf)
    offset = first_call - plf
    gate = (1.0 / (1.0 + 4.0 * offset * offset)).astype(jnp.bfloat16)

    across = send(gate, half, count)
    direct = {k: send(pick(gate, wants[k][0]), k, count) for k in wants}
    passed = {k: send(pick(across, wants[k][1]), k, count) for k in wants}
    far = [pick(gate, choice[0])]
    far += [direct[k] for k in wants]
    far += [pick(across, choice[half])]
    far += [passed[k] for k in wants]
    far_gate = jnp.concatenate(far, axis=0)
    far_f = far_gate.astype(jnp.float32)
    far_cov = (far_f * near_cov.astype(jnp.float32)).astype(jnp.bfloat16)
    far_sq = (far_f * near_sq.astype(jnp.float32)).astype(jnp.bfloat16)
    ref_mean, rel_var = spread_terms(
        weighted(weight_map, far_gate), weighted(weight_map, far_cov), weighted(weight_map, far_sq)
    )
    return copy_calls(normf, ref_mean, rel_var, plf)


def solution(mesh):
    in_specs = (
        P("samp", ("slab", "tgt")),
        P("samp", None),
        P("samp", None),
        P("samp"),
        P(("slab", "tgt")),
    )
    out_specs = P("samp", ("slab", "tgt"))
    return jax.shard_map(body, mesh=mesh, in_specs=in_specs, out_specs=out_specs, check_vma=False)
```

```python
import functools

import jax
import jax.numpy as jnp
from jax import lax
from jax.experimental import pallas as pl
from jax.experimental.pallas import tpu as pltpu
from jax.sharding import PartitionSpec as P

NGC = 8
RBLK = 128
LANE = 128
CHUNK = 32
GROUP = 8

LOG_PRIOR = (-4.6051702, -3.2188758, -0.1625189, -2.8134107, -3.5065579, -4.6051702)

F32 = jnp.float32
BF16 = jnp.bfloat16
EXACT = lax.Precision.HIGHEST


def swap_tgt(value):
    return lax.ppermute(value, "tgt", [(0, 1), (1, 0)])


def send(value, step, count):
    return lax.ppermute(value, "samp", [(i, i ^ step) for i in range(count)])


def call(body, name, outs, *args, scratch=()):
    return pl.pallas_call(
        body,
        out_shape=[jax.ShapeDtypeStruct(shape, dtype) for shape, dtype in outs],
        in_specs=[pl.BlockSpec(memory_space=pltpu.VMEM)] * len(args),
        out_specs=[pl.BlockSpec(memory_space=pltpu.VMEM)] * len(outs),
        scratch_shapes=list(scratch),
        compiler_params=pltpu.CompilerParams(vmem_limit_bytes=16 * 2**20),
        name=name,
    )(*args)


def dot(left, right, left_dim, right_dim, precision=None):
    return lax.dot_general(
        left,
        right,
        (((left_dim,), (right_dim,)), ((), ())),
        precision=precision,
        preferred_element_type=F32,
    )


def pick(ref, ask, parts):
    chosen = ref[0:RBLK]
    for part in range(1, parts):
        chosen = jnp.where(ask == part, ref[part * RBLK : (part + 1) * RBLK], chosen)
    return chosen


def ask_kernel(neighbours, coverage, noted, ask):
    rows, cols = coverage.shape
    index = neighbours[...]
    position = lax.div(index, rows) ^ lax.axis_index("samp")
    block = lax.div(lax.rem(index, rows), RBLK)
    count = lax.axis_size("samp")
    best = [
        jnp.max(jnp.where(position == p, block, 0), axis=0, keepdims=True) for p in range(count)
    ]
    best += [jnp.zeros_like(best[0])] * (ask.shape[0] - count)
    best = jnp.max(jnp.concatenate(best, axis=0), axis=1, keepdims=True)
    wide = jnp.broadcast_to(best.astype(F32), ask.shape).astype(BF16)
    ask[...] = wide
    noted[0:rows] = coverage[...]
    noted[rows:] = wide


def map_kernel(neighbours, weight, ask, out, total, wide):
    rows = neighbours.shape[0]
    listed = neighbours.shape[1]
    count = lax.axis_size("samp")
    me = lax.axis_index("samp")
    sample = lax.broadcasted_iota(jnp.int32, (RBLK, listed), 0).astype(F32).astype(BF16)
    device = lax.broadcasted_iota(jnp.int32, (count, listed), 0)
    one, zero = jnp.ones((), BF16), jnp.zeros((), BF16)

    def step(i, carry):
        start = pl.multiple_of(i * GROUP, GROUP)
        index = neighbours[pl.ds(start, GROUP), :]
        heavy = weight[pl.ds(start, GROUP), :].astype(F32)
        position = lax.div(index, rows) ^ me
        low = lax.rem(index, RBLK).astype(F32).astype(BF16)
        for r in range(0, GROUP, 2):
            low_one = jnp.concatenate(
                [jnp.where(sample == low[q : q + 1], one, zero) for q in (r, r + 1)], axis=1
            )
            high = [
                jnp.where(device == position[q : q + 1], heavy[q : q + 1], 0.0) for q in (r, r + 1)
            ]
            none = jnp.zeros_like(high[0])
            high_one = jnp.concatenate(
                [jnp.concatenate([high[0], none], axis=1), jnp.concatenate([none, high[1]], axis=1)],
                axis=0,
            ).astype(BF16)
            both = dot(high_one, low_one, 1, 1)
            wide[:, pl.ds(start + r, 1), :] = both[:count].reshape(count, 1, RBLK)
            wide[:, pl.ds(start + r + 1, 1), :] = both[count:].reshape(count, 1, RBLK)
        return carry

    lax.fori_loop(0, rows // GROUP, step, 0, unroll=8)
    for p in range(count):
        out[:, p * RBLK : (p + 1) * RBLK] = wide[p].astype(BF16)
    summed = jnp.sum(weight[...].astype(F32), axis=1, keepdims=True)
    total[...] = jnp.broadcast_to(summed, total.shape)


def bin_rows(gc):
    return (lax.broadcasted_iota(jnp.int32, (NGC, gc.shape[1]), 0) == gc[...]).astype(F32)


def bin_sums(onehot, block):
    return dot(onehot.astype(BF16), block, 1, 1)


def factors(sums, number, targets):
    mean = jnp.sum(sums, axis=0, keepdims=True) / targets
    scale = mean / (sums / jnp.maximum(number, 1.0))
    return jnp.where(sums > 0, scale, 0.0)


def normal(block, scale, onehot):
    return (block.astype(F32) * dot(scale, onehot, 0, 0, EXACT)).astype(BF16)


def stats_kernel(coverage, across, gc, stats):
    rows = coverage.shape[0]
    onehot = bin_rows(gc)
    stats[:, 0:rows] = bin_sums(onehot, coverage[...])
    stats[:, rows : 2 * rows] = bin_sums(onehot, across[0:rows])
    number = jnp.sum(onehot, axis=1, keepdims=True)
    stats[:, 2 * rows :] = jnp.broadcast_to(number, (NGC, LANE))


def norm_kernel(half, coverage, across, mine, theirs, gc, ask, *refs):
    noted, refs = refs[: half - 1], refs[half - 1 :]
    own, near, far, raw, sums = refs[:5]
    passed = refs[5:]
    rows, cols = coverage.shape
    parts = rows // RBLK
    targets = cols * lax.axis_size("tgt")
    onehot = bin_rows(gc)
    number = mine[:, 2 * rows : 2 * rows + 1] + theirs[:, 2 * rows : 2 * rows + 1]
    scale = factors(mine[:, 0 : 2 * rows] + theirs[:, 0 : 2 * rows], number, targets)
    own[...] = normal(coverage[...], scale[:, 0:rows], onehot)
    far[...] = normal(across[0:rows], scale[:, rows : 2 * rows], onehot)
    near[0:RBLK] = pick(own, ask[0:1], parts)
    near[RBLK : 2 * RBLK] = pick(far, ask[half : half + 1], parts)
    for k in range(1, half):
        note = noted[k - 1]
        other = k ^ half
        passed[k - 1][0:RBLK] = pick(far, note[rows + other : rows + other + 1], parts)
        passed[k - 1][RBLK:] = across[rows:]
        place = pl.ds((k - 1) * RBLK, RBLK)
        raw[place, :] = pick(note, ask[k : k + 1], parts)
        sums[:, (k - 1) * RBLK : k * RBLK] = bin_sums(onehot, raw[place, :])


def spread(first, second, third, normf, ratio, rel, part):
    mean = second / first
    inverse = 1.0 / mean
    ratio[...] = normf * inverse
    relative = (third / first) * (inverse * inverse) - 1.0
    rel[...] = relative
    part[...] = dot(jnp.ones((NGC, relative.shape[1]), F32), relative, 1, 1, EXACT)


def squared(block):
    wide = block.astype(F32)
    return (wide * wide).astype(BF16)


def first_kernel(half, weight, total, own, near, raw, sums, sums_two, mine, theirs, gc, *refs):
    passed, refs = refs[: half - 1], refs[half - 1 :]
    table, ratio, rel, part = refs
    rows, cols = own.shape
    onehot = bin_rows(gc)
    number = mine[:, 2 * rows : 2 * rows + 1] + theirs[:, 2 * rows : 2 * rows + 1]
    scale = factors(sums[...] + sums_two[...], number, cols * lax.axis_size("tgt"))
    table[0:RBLK] = near[0:RBLK]
    table[half * RBLK : (half + 1) * RBLK] = near[RBLK : 2 * RBLK]
    table[RBLK : half * RBLK] = normal(raw[...], scale, onehot)
    for k in range(1, half):
        other = k ^ half
        table[other * RBLK : (other + 1) * RBLK] = passed[k - 1][0:RBLK]
    second = dot(weight[...], table[...], 1, 0)
    third = dot(weight[...], squared(table[...]), 1, 0)
    first = jnp.concatenate([total[...]] * (cols // LANE), axis=1)
    spread(first, second, third, own[...].astype(F32), ratio, rel, part)


def second_kernel(count, weight, table, own, gate, ask, *refs):
    arrived, refs = refs[: count - 1], refs[count - 1 :]
    ratio, rel, part = refs
    rows, cols = own.shape
    gates = [pick(gate, ask[0:1], rows // RBLK)] + [ref[...] for ref in arrived]
    gates = jnp.concatenate(gates, axis=0)
    wide = gates.astype(F32)
    covs = (wide * table[...].astype(F32)).astype(BF16)
    squares = (wide * squared(table[...]).astype(F32)).astype(BF16)
    first = dot(weight[...], gates, 1, 0)
    second = dot(weight[...], covs, 1, 0)
    third = dot(weight[...], squares, 1, 0)
    spread(first, second, third, own[...].astype(F32), ratio, rel, part)


def called(ratio, rel, part, part_two, plf, finish):
    rows, cols = ratio.shape
    targets = cols * lax.axis_size("tgt")
    at_top = (lax.broadcasted_iota(jnp.int32, (NGC, LANE), 0) == 0).astype(F32)
    level_part = dot((part[...] + part_two[...]) * (0.5 / targets), at_top, 0, 0, EXACT)
    for start in range(0, rows, CHUNK):
        here = slice(start, start + CHUNK)
        shared = level_part[here]
        ploidy = plf[here]
        for lane in range(0, cols, LANE):
            there = slice(lane, lane + LANE)
            level = 0.5 * rel[here, there] + shared
            copies = ratio[here, there]
            scores, roots = [], []
            for state, prior in enumerate(LOG_PRIOR):
                centre = max(state, 0.1) / ploidy
                root = lax.rsqrt(level * jnp.maximum(centre, 0.25) + 0.01)
                delta = (copies - centre) * root
                scores.append(prior - 0.5 * (delta * delta))
                roots.append(root)
            peak = functools.reduce(jnp.maximum, scores)
            expo = [jnp.exp(s - peak) * root for s, root in zip(scores, roots)]
            top = expo[1]
            for state in range(2, 6):
                top = top + float(state) * expo[state]
            finish(here, there, top / functools.reduce(jnp.add, expo), ploidy)


def gate_kernel(half, parts, ratio, rel, part, part_two, plf, across, *refs):
    count = 2 * half
    rows = ratio.shape[0]
    noted, passed, refs = refs[: half - 1], refs[half - 1 : 2 * half - 2], refs[2 * half - 2 :]
    gate, out = refs[0], refs[1:]

    def finish(here, there, value, ploidy):
        offset = value - ploidy
        gate[here, there] = (1.0 / (1.0 + 4.0 * (offset * offset))).astype(BF16)

    called(ratio, rel, part, part_two, plf, finish)
    for p in range(1, count):
        if p < half:
            ask = noted[p - 1][rows + p : rows + p + 1]
        elif p == half:
            ask = across[rows + p : rows + p + 1]
        else:
            ask = passed[(p ^ half) - 1][RBLK + p : RBLK + p + 1]
        out[p - 1][...] = pick(gate, ask, parts)


def final_kernel(ratio, rel, part, part_two, plf, out):
    def finish(here, there, value, ploidy):
        out[here, there] = value

    called(ratio, rel, part, part_two, plf, finish)


def body(coverage, neighbours, nbr_weight, ploidy, gc_bin):
    count = lax.axis_size("samp")
    half = count // 2
    mates = range(1, half)
    rows, cols = coverage.shape
    listed = neighbours.shape[1]
    parts = rows // RBLK
    extra = -(-count // 16) * 16
    gc = gc_bin.reshape(1, cols)
    plf = jnp.broadcast_to(ploidy.astype(F32)[:, None], (rows, LANE))

    noted, ask = call(
        ask_kernel, "choices", [((rows + extra, cols), BF16), ((extra, cols), BF16)],
        neighbours, coverage,
    )
    across = send(noted, half, count)
    noted = [send(noted, k, count) for k in mates]
    weight, total = call(
        map_kernel, "weight_map", [((rows, count * RBLK), BF16), ((rows, LANE), F32)],
        neighbours, nbr_weight, ask, scratch=[pltpu.VMEM((count, rows, RBLK), F32)],
    )
    (mine,) = call(
        stats_kernel, "bin_sums", [((NGC, 2 * rows + LANE), F32)], coverage, across, gc
    )
    theirs = swap_tgt(mine)
    own, near, _, raw, sums, *passed = call(
        functools.partial(norm_kernel, half), "normalise",
        [
            ((rows, cols), BF16),
            ((2 * RBLK, cols), BF16),
            ((rows, cols), BF16),
            ((len(mates) * RBLK, cols), BF16),
            ((NGC, len(mates) * RBLK), F32),
        ] + [((RBLK + extra, cols), BF16)] * len(mates),
        coverage, across, mine, theirs, gc, ask, *noted,
    )
    passed = [send(block, k, count) for k, block in zip(mates, passed)]
    sums_two = swap_tgt(sums)
    table, ratio, rel, part = call(
        functools.partial(first_kernel, half), "moments_one",
        [
            ((count * RBLK, cols), BF16),
            ((rows, cols), F32),
            ((rows, cols), F32),
            ((NGC, rows), F32),
        ],
        weight, total, own, near, raw, sums, sums_two, mine, theirs, gc, *passed,
    )
    gate, *gates = call(
        functools.partial(gate_kernel, half, parts), "gate",
        [((rows, cols), BF16)] + [((RBLK, cols), BF16)] * (count - 1),
        ratio, rel, part, swap_tgt(part), plf, across, *noted, *passed,
    )
    gates = [send(block, p, count) for p, block in enumerate(gates, 1)]
    ratio, rel, part = call(
        functools.partial(second_kernel, count), "moments_two",
        [((rows, cols), F32), ((rows, cols), F32), ((NGC, rows), F32)],
        weight, table, own, gate, ask, *gates,
    )
    (out,) = call(
        final_kernel, "copy_number", [((rows, cols), F32)], ratio, rel, part, swap_tgt(part), plf
    )
    return out


def solution(mesh):
    in_specs = (
        P("samp", ("slab", "tgt")),
        P("samp", None),
        P("samp", None),
        P("samp"),
        P(("slab", "tgt")),
    )
    out_specs = P("samp", ("slab", "tgt"))
    return jax.shard_map(body, mesh=mesh, in_specs=in_specs, out_specs=out_specs, check_vma=False)
```

```python
import functools

import jax
import jax.numpy as jnp
from jax import lax
from jax.experimental import pallas as pl
from jax.experimental.pallas import tpu as pltpu
from jax.sharding import PartitionSpec as P

NGC = 8
RBLK = 128
LANE = 128
CHUNK = 32
GROUP = 8

LOG_PRIOR = (-4.6051702, -3.2188758, -0.1625189, -2.8134107, -3.5065579, -4.6051702)

F32 = jnp.float32
BF16 = jnp.bfloat16
EXACT = lax.Precision.HIGHEST


def swap_tgt(value):
    return lax.ppermute(value, "tgt", [(0, 1), (1, 0)])


def send(value, step, count):
    return lax.ppermute(value, "samp", [(i, i ^ step) for i in range(count)])


def call(body, name, outs, *args, scratch=()):
    return pl.pallas_call(
        body,
        out_shape=[jax.ShapeDtypeStruct(shape, dtype) for shape, dtype in outs],
        in_specs=[pl.BlockSpec(memory_space=pltpu.VMEM)] * len(args),
        out_specs=[pl.BlockSpec(memory_space=pltpu.VMEM)] * len(outs),
        scratch_shapes=list(scratch),
        compiler_params=pltpu.CompilerParams(vmem_limit_bytes=16 * 2**20),
        name=name,
    )(*args)


def dot(left, right, left_dim, right_dim, precision=None):
    return lax.dot_general(
        left,
        right,
        (((left_dim,), (right_dim,)), ((), ())),
        precision=precision,
        preferred_element_type=F32,
    )


def pick(ref, ask, parts):
    chosen = ref[0:RBLK]
    for part in range(1, parts):
        chosen = jnp.where(ask == part, ref[part * RBLK : (part + 1) * RBLK], chosen)
    return chosen


def ask_kernel(rows, neighbours, ask):
    index = neighbours[...]
    position = lax.div(index, rows) ^ lax.axis_index("samp")
    block = lax.div(lax.rem(index, rows), RBLK)
    count = lax.axis_size("samp")
    best = [
        jnp.max(jnp.where(position == p, block, 0), axis=0, keepdims=True) for p in range(count)
    ]
    best += [jnp.zeros_like(best[0])] * (ask.shape[0] - count)
    best = jnp.max(jnp.concatenate(best, axis=0), axis=1, keepdims=True)
    ask[...] = jnp.broadcast_to(best.astype(F32), ask.shape).astype(BF16)


def map_kernel(neighbours, weight, plf, noted, out, total, wide):
    rows = neighbours.shape[0]
    listed = neighbours.shape[1]
    count = lax.axis_size("samp")
    me = lax.axis_index("samp")
    sample = lax.broadcasted_iota(jnp.int32, (RBLK, listed), 0).astype(F32).astype(BF16)
    device = lax.broadcasted_iota(jnp.int32, (count, listed), 0)
    one, zero = jnp.ones((), BF16), jnp.zeros((), BF16)

    def step(i, carry):
        start = pl.multiple_of(i * GROUP, GROUP)
        index = neighbours[pl.ds(start, GROUP), :]
        heavy = weight[pl.ds(start, GROUP), :].astype(F32)
        position = lax.div(index, rows) ^ me
        low = lax.rem(index, RBLK).astype(F32).astype(BF16)
        for r in range(0, GROUP, 2):
            low_one = jnp.concatenate(
                [jnp.where(sample == low[q : q + 1], one, zero) for q in (r, r + 1)], axis=1
            )
            high = [
                jnp.where(device == position[q : q + 1], heavy[q : q + 1], 0.0) for q in (r, r + 1)
            ]
            none = jnp.zeros_like(high[0])
            high_one = jnp.concatenate(
                [jnp.concatenate([high[0], none], axis=1), jnp.concatenate([none, high[1]], axis=1)],
                axis=0,
            ).astype(BF16)
            both = dot(high_one, low_one, 1, 1)
            wide[:, pl.ds(start + r, 1), :] = both[:count].reshape(count, 1, RBLK)
            wide[:, pl.ds(start + r + 1, 1), :] = both[count:].reshape(count, 1, RBLK)
        return carry

    lax.fori_loop(0, rows // GROUP, step, 0, unroll=8)
    for p in range(count):
        out[:, p * RBLK : (p + 1) * RBLK] = wide[p].astype(BF16)
    summed = jnp.sum(weight[...].astype(F32), axis=1, keepdims=True)
    total[...] = jnp.broadcast_to(summed, total.shape)


def bin_rows(gc):
    return (lax.broadcasted_iota(jnp.int32, (NGC, gc.shape[1]), 0) == gc[...]).astype(F32)


def stats_kernel(coverage, gc, stats):
    rows = coverage.shape[0]
    onehot = bin_rows(gc)
    stats[:, 0:rows] = dot(onehot.astype(BF16), coverage[...], 1, 1)
    number = jnp.sum(onehot, axis=1, keepdims=True)
    stats[:, rows:] = jnp.broadcast_to(number, (NGC, LANE))


def norm_kernel(coverage, mine, theirs, gc, ask, noted):
    rows, cols = coverage.shape
    onehot = bin_rows(gc)
    sums = mine[:, 0:rows] + theirs[:, 0:rows]
    number = mine[:, rows : rows + 1] + theirs[:, rows : rows + 1]
    mean = jnp.sum(sums, axis=0, keepdims=True) / (cols * lax.axis_size("tgt"))
    scale = mean / (sums / jnp.maximum(number, 1.0))
    scale = dot(jnp.where(sums > 0, scale, 0.0), onehot, 0, 0, EXACT)
    noted[0:rows] = (coverage[...].astype(F32) * scale).astype(BF16)
    noted[rows:] = ask[...]


def pass_kernel(relay, asked, total, across, *refs):
    mates = len(refs) // 2
    half = mates + 1
    noted, out = refs[:mates], refs[mates:]
    rows = across.shape[0] - asked
    parts = rows // RBLK
    for k in range(1, half):
        note = noted[k - 1]
        base = note.shape[0] - asked
        other = base + (k ^ half)
        out[k - 1][0:RBLK] = pick(across, note[other : other + 1], parts)
        last = RBLK
        if relay and k == 1:
            out[0][RBLK : 2 * RBLK] = pick(noted[1], note[base + 3 : base + 4], parts)
            last = 2 * RBLK
        out[k - 1][last:] = across[rows:]


def spread(first, second, third, normf, ratio, rel, part):
    mean = second / first
    inverse = 1.0 / mean
    ratio[...] = normf * inverse
    relative = (third / first) * (inverse * inverse) - 1.0
    rel[...] = relative
    part[...] = dot(jnp.ones((NGC, relative.shape[1]), F32), relative, 1, 1, EXACT)


def squared(block):
    wide = block.astype(F32)
    return (wide * wide).astype(BF16)


def first_kernel(relay, rows, weight, total, own, across, ask, *refs):
    mates = (len(refs) - 4) // 2
    half = mates + 1
    noted, passed, (table, ratio, rel, part) = refs[:mates], refs[mates : 2 * mates], refs[2 * mates :]
    cols = own.shape[1]
    parts = rows // RBLK
    table[0:RBLK] = pick(own, ask[0:1], parts)
    table[half * RBLK : (half + 1) * RBLK] = pick(across, ask[half : half + 1], parts)
    for k in range(1, half):
        if relay and k == 3:
            here = passed[0][RBLK : 2 * RBLK]
        else:
            here = pick(noted[k - 1], ask[k : k + 1], parts)
        table[k * RBLK : (k + 1) * RBLK] = here
        other = k ^ half
        table[other * RBLK : (other + 1) * RBLK] = passed[k - 1][0:RBLK]
    second = dot(weight[...], table[...], 1, 0)
    third = dot(weight[...], squared(table[...]), 1, 0)
    first = jnp.concatenate([total[...]] * (cols // LANE), axis=1)
    spread(first, second, third, own[0:rows].astype(F32), ratio, rel, part)


def second_kernel(order, weight, table, own, gate, ask, *refs):
    count = len(order) + 1
    arrived = [refs[order.index(p)] for p in range(1, count)]
    refs = refs[count - 1 :]
    ratio, rel, part = refs
    rows, cols = gate.shape
    gates = [pick(gate, ask[0:1], rows // RBLK)] + [ref[...] for ref in arrived]
    gates = jnp.concatenate(gates, axis=0)
    wide = gates.astype(F32)
    covs = (wide * table[...].astype(F32)).astype(BF16)
    squares = (wide * squared(table[...]).astype(F32)).astype(BF16)
    first = dot(weight[...], gates, 1, 0)
    second = dot(weight[...], covs, 1, 0)
    third = dot(weight[...], squares, 1, 0)
    spread(first, second, third, own[0:rows].astype(F32), ratio, rel, part)


def called(ratio, rel, part, part_two, plf, finish):
    rows, cols = ratio.shape
    targets = cols * lax.axis_size("tgt")
    at_top = (lax.broadcasted_iota(jnp.int32, (NGC, LANE), 0) == 0).astype(F32)
    level_part = dot((part[...] + part_two[...]) * (0.5 / targets), at_top, 0, 0, EXACT)
    for start in range(0, rows, CHUNK):
        here = slice(start, start + CHUNK)
        shared = level_part[here]
        ploidy = plf[here]
        for lane in range(0, cols, LANE):
            there = slice(lane, lane + LANE)
            level = 0.5 * rel[here, there] + shared
            copies = ratio[here, there]
            scores, roots = [], []
            for state, prior in enumerate(LOG_PRIOR):
                centre = max(state, 0.1) / ploidy
                root = lax.rsqrt(level * jnp.maximum(centre, 0.25) + 0.01)
                delta = (copies - centre) * root
                scores.append(prior - 0.5 * (delta * delta))
                roots.append(root)
            peak = functools.reduce(jnp.maximum, scores)
            expo = [jnp.exp(s - peak) * root for s, root in zip(scores, roots)]
            top = expo[1]
            for state in range(2, 6):
                top = top + float(state) * expo[state]
            finish(here, there, top / functools.reduce(jnp.add, expo), ploidy)


def gate_kernel(asked, ratio, rel, part, part_two, plf, across, *refs):
    rows = ratio.shape[0]
    mates = (len(refs) - 2) // 4
    half = mates + 1
    noted, passed, gate, out = refs[:mates], refs[mates : 2 * mates], refs[2 * mates], refs[2 * mates + 1 :]

    def finish(here, there, value, ploidy):
        offset = value - ploidy
        gate[here, there] = (1.0 / (1.0 + 4.0 * (offset * offset))).astype(BF16)

    called(ratio, rel, part, part_two, plf, finish)
    for p in range(1, 2 * half):
        if p < half:
            source = noted[p - 1]
        elif p == half:
            source = across
        else:
            source = passed[(p ^ half) - 1]
        place = source.shape[0] - asked + p
        out[p - 1][...] = pick(gate, source[place : place + 1], rows // RBLK)


def final_kernel(ratio, rel, part, part_two, plf, out):
    def finish(here, there, value, ploidy):
        out[here, there] = value

    called(ratio, rel, part, part_two, plf, finish)


def body(coverage, neighbours, nbr_weight, ploidy, gc_bin):
    count = lax.axis_size("samp")
    half = count // 2
    mates = range(1, half)
    rows, cols = coverage.shape
    extra = -(-count // 16) * 16
    relay = half > 3
    gc = gc_bin.reshape(1, cols)
    plf = jnp.broadcast_to(ploidy.astype(F32)[:, None], (rows, LANE))

    (mine,) = call(stats_kernel, "bin_sums", [((NGC, rows + LANE), F32)], coverage, gc)
    theirs = swap_tgt(mine)
    (ask,) = call(
        functools.partial(ask_kernel, rows), "choices", [((extra, cols), BF16)], neighbours
    )
    (own,) = call(
        norm_kernel, "normalise", [((rows + extra, cols), BF16)], coverage, mine, theirs, gc, ask
    )
    across = send(own, half, count)
    noted = [send(ask if relay and k == 3 else own, k, count) for k in mates]
    weight, total = call(
        map_kernel, "weight_map", [((rows, count * RBLK), BF16), ((rows, LANE), F32)],
        neighbours, nbr_weight, plf, own, scratch=[pltpu.VMEM((count, rows, RBLK), F32)],
    )
    passed = call(
        functools.partial(pass_kernel, relay, extra), "pass_on",
        [(((2 if relay and k == 1 else 1) * RBLK + extra, cols), BF16) for k in mates],
        total, across, *noted,
    )
    passed = [send(block, k, count) for k, block in zip(mates, passed)]
    table, ratio, rel, part = call(
        functools.partial(first_kernel, relay, rows), "moments_one",
        [
            ((count * RBLK, cols), BF16),
            ((rows, cols), F32),
            ((rows, cols), F32),
            ((NGC, rows), F32),
        ],
        weight, total, own, across, ask, *noted, *passed,
    )
    gate, *gates = call(
        functools.partial(gate_kernel, extra), "gate",
        [((rows, cols), BF16)] + [((RBLK, cols), BF16)] * (count - 1),
        ratio, rel, part, swap_tgt(part), plf, across, *noted, *passed,
    )
    order = [(half - 1 - i // 2) ^ (half if i % 2 == 0 else 0) for i in range(count)]
    order = [p for p in order if p]
    gates = [send(gates[p - 1], p, count) for p in order]
    ratio, rel, part = call(
        functools.partial(second_kernel, order), "moments_two",
        [((rows, cols), F32), ((rows, cols), F32), ((NGC, rows), F32)],
        weight, table, own, gate, ask, *gates,
    )
    (out,) = call(
        final_kernel, "copy_number", [((rows, cols), F32)], ratio, rel, part, swap_tgt(part), plf
    )
    return out


def solution(mesh):
    in_specs = (
        P("samp", ("slab", "tgt")),
        P("samp", None),
        P("samp", None),
        P("samp"),
        P(("slab", "tgt")),
    )
    out_specs = P("samp", ("slab", "tgt"))
    return jax.shard_map(body, mesh=mesh, in_specs=in_specs, out_specs=out_specs, check_vma=False)
```

```python
import functools
import math

import jax
import jax.numpy as jnp
from jax import lax
from jax.experimental import pallas as pl
from jax.experimental.pallas import tpu as pltpu
from jax.sharding import PartitionSpec as P

NGC = 8
RBLK = 128
LANE = 128
CHUNK = 32
GROUP = 8

LOG_PRIOR = (-4.6051702, -3.2188758, -0.1625189, -2.8134107, -3.5065579, -4.6051702)

F32 = jnp.float32
BF16 = jnp.bfloat16
EXACT = lax.Precision.HIGHEST


def swap_tgt(value):
    return lax.ppermute(value, "tgt", [(0, 1), (1, 0)])


def send(value, step, count):
    return lax.ppermute(value, "samp", [(i, i ^ step) for i in range(count)])


def call(body, name, outs, *args, scratch=(), cost=1):
    return pl.pallas_call(
        body,
        out_shape=[jax.ShapeDtypeStruct(shape, dtype) for shape, dtype in outs],
        in_specs=[pl.BlockSpec(memory_space=pltpu.VMEM)] * len(args),
        out_specs=[pl.BlockSpec(memory_space=pltpu.VMEM)] * len(outs),
        scratch_shapes=list(scratch),
        compiler_params=pltpu.CompilerParams(vmem_limit_bytes=16 * 2**20),
        cost_estimate=pl.CostEstimate(flops=cost, bytes_accessed=cost, transcendentals=0),
        name=name,
    )(*args)


def dot(left, right, left_dim, right_dim, precision=None):
    return lax.dot_general(
        left,
        right,
        (((left_dim,), (right_dim,)), ((), ())),
        precision=precision,
        preferred_element_type=F32,
    )


def pick(ref, ask, parts):
    chosen = ref[0:RBLK]
    for part in range(1, parts):
        chosen = jnp.where(ask == part, ref[part * RBLK : (part + 1) * RBLK], chosen)
    return chosen


def ask_kernel(rows, neighbours, ask):
    index = neighbours[...]
    position = lax.div(index, rows) ^ lax.axis_index("samp")
    block = lax.div(lax.rem(index, rows), RBLK)
    count = lax.axis_size("samp")
    best = [
        jnp.max(jnp.where(position == p, block, 0), axis=0, keepdims=True) for p in range(count)
    ]
    best += [jnp.zeros_like(best[0])] * (ask.shape[0] - count)
    best = jnp.max(jnp.concatenate(best, axis=0), axis=1, keepdims=True)
    ask[...] = jnp.broadcast_to(best.astype(F32), ask.shape).astype(BF16)


def map_kernel(neighbours, weight, plf, noted, out, total, wide):
    rows = neighbours.shape[0]
    listed = neighbours.shape[1]
    count = lax.axis_size("samp")
    me = lax.axis_index("samp")
    sample = lax.broadcasted_iota(jnp.int32, (RBLK, listed), 0).astype(F32).astype(BF16)
    device = lax.broadcasted_iota(jnp.int32, (count, listed), 0)
    one, zero = jnp.ones((), BF16), jnp.zeros((), BF16)

    def step(i, carry):
        start = pl.multiple_of(i * GROUP, GROUP)
        index = neighbours[pl.ds(start, GROUP), :]
        heavy = weight[pl.ds(start, GROUP), :].astype(F32)
        position = lax.div(index, rows) ^ me
        low = lax.rem(index, RBLK).astype(F32).astype(BF16)
        for r in range(0, GROUP, 2):
            low_one = jnp.concatenate(
                [jnp.where(sample == low[q : q + 1], one, zero) for q in (r, r + 1)], axis=1
            )
            high = [
                jnp.where(device == position[q : q + 1], heavy[q : q + 1], 0.0) for q in (r, r + 1)
            ]
            none = jnp.zeros_like(high[0])
            high_one = jnp.concatenate(
                [jnp.concatenate([high[0], none], axis=1), jnp.concatenate([none, high[1]], axis=1)],
                axis=0,
            ).astype(BF16)
            both = dot(high_one, low_one, 1, 1)
            wide[:, pl.ds(start + r, 1), :] = both[:count].reshape(count, 1, RBLK)
            wide[:, pl.ds(start + r + 1, 1), :] = both[count:].reshape(count, 1, RBLK)
        return carry

    lax.fori_loop(0, rows // GROUP, step, 0, unroll=8)
    for p in range(count):
        out[:, p * RBLK : (p + 1) * RBLK] = wide[p].astype(BF16)
    summed = jnp.sum(weight[...].astype(F32), axis=1, keepdims=True)
    total[...] = jnp.broadcast_to(summed, total.shape)


def stats_kernel(coverage, onehot, stats):
    rows = coverage.shape[0]
    stats[:, 0:rows] = dot(onehot[...].astype(BF16), coverage[...], 1, 1)
    number = jnp.sum(onehot[...], axis=1, keepdims=True)
    stats[:, rows:] = jnp.broadcast_to(number, (NGC, LANE))


def norm_kernel(coverage, mine, theirs, onehot, ask, noted, wide):
    rows, cols = coverage.shape
    extra = ask.shape[0]
    sums = mine[:, 0:rows] + theirs[:, 0:rows]
    number = mine[:, rows : rows + 1] + theirs[:, rows : rows + 1]
    mean = jnp.sum(sums, axis=0, keepdims=True) / (cols * lax.axis_size("tgt"))
    scale = mean / (sums / jnp.maximum(number, 1.0))
    scale = dot(jnp.where(sums > 0, scale, 0.0), onehot[...], 0, 0, EXACT)
    block = (coverage[...].astype(F32) * scale).astype(BF16)
    for out in (noted, wide):
        out[0:rows] = block
        out[rows : rows + extra] = ask[...]
    wide[rows + extra :] = ask[...]


def pass_kernel(late, asked, total, own, across, *refs):
    mates = len(refs) // 2
    half = mates + 1
    noted, out = refs[:mates], refs[mates:]
    rows = own.shape[0] - asked
    parts = rows // RBLK
    for k in range(1, half):
        note = noted[k - 1]
        base = note.shape[0] - asked
        other = base + (k ^ half)
        out[k - 1][0:RBLK] = pick(across, note[other : other + 1], parts)
        if k in late:
            out[k - 1][RBLK : 2 * RBLK] = pick(own, note[base + k : base + k + 1], parts)
        out[k - 1][out[k - 1].shape[0] - asked :] = across[rows : rows + asked]


def spread(first, second, third, normf, ratio, rel, own_sum, part):
    inverse = 1.0 / second
    scaled = first * inverse
    ratio[...] = normf * scaled
    relative = (third * inverse) * scaled - 1.0
    rel[...] = relative
    own_sum[...] = jnp.broadcast_to(jnp.sum(relative, axis=1, keepdims=True), own_sum.shape)
    for start in range(0, own_sum.shape[0], LANE):
        block = jnp.where(diagonal(), own_sum[start : start + LANE], 0.0)
        part[:, start : start + LANE] = jnp.sum(block, axis=0, keepdims=True)


def diagonal():
    row = lax.broadcasted_iota(jnp.int32, (LANE, LANE), 0)
    return row == lax.broadcasted_iota(jnp.int32, (LANE, LANE), 1)


def squared(block):
    wide = block.astype(F32)
    return (wide * wide).astype(BF16)


def columns(weight, positions):
    return jnp.concatenate([weight[:, p * RBLK : (p + 1) * RBLK] for p in positions], axis=1)


def place(table, positions):
    return jnp.concatenate([table[p * RBLK : (p + 1) * RBLK] for p in positions], axis=0)


def early_one_kernel(early, rows, weight, own, across, ask, *refs):
    noted, (table, partial) = refs[:-2], refs[-2:]
    parts = rows // RBLK
    half = len(noted) + 1
    for p in early:
        source = own if p == 0 else across if p == half else noted[p - 1]
        table[p * RBLK : (p + 1) * RBLK] = pick(source, ask[p : p + 1], parts)
    mine, block = columns(weight, early), place(table, early)
    partial[0] = dot(mine, block, 1, 0)
    partial[1] = dot(mine, squared(block), 1, 0)


def first_kernel(late, rows, weight, total, own, early, partial, *refs):
    mates = len(refs) - 5
    half = mates + 1
    passed, (table, ratio, rel, own_sum, part) = refs[:mates], refs[mates:]
    cols = own.shape[1]
    table[...] = early[...]
    arrived = []
    for k in range(1, half):
        if k in late:
            arrived.append(k)
            table[k * RBLK : (k + 1) * RBLK] = passed[k - 1][RBLK : 2 * RBLK]
        other = k ^ half
        arrived.append(other)
        table[other * RBLK : (other + 1) * RBLK] = passed[k - 1][0:RBLK]
    mine, block = columns(weight, arrived), place(table, arrived)
    second = partial[0] + dot(mine, block, 1, 0)
    third = partial[1] + dot(mine, squared(block), 1, 0)
    first = jnp.concatenate([total[...]] * (cols // LANE), axis=1)
    spread(first, second, third, own[0:rows].astype(F32), ratio, rel, own_sum, part)


def gated(weight, table, gates, positions):
    mine, block = columns(weight, positions), place(table, positions)
    wide = gates.astype(F32)
    covs = (wide * block.astype(F32)).astype(BF16)
    squares = (wide * squared(block).astype(F32)).astype(BF16)
    return [dot(mine, values, 1, 0) for values in (gates, covs, squares)]


def early_two_kernel(early, weight, table, gate, ask, *refs):
    arrived, partial = refs[:-1], refs[-1]
    own = pick(gate, ask[0:1], gate.shape[0] // RBLK)
    gates = jnp.concatenate([own] + [ref[...] for ref in arrived], axis=0)
    for i, moment in enumerate(gated(weight, table, gates, [0] + early)):
        partial[i] = moment


def second_kernel(late, rows, weight, table, own, partial, *refs):
    arrived, (ratio, rel, own_sum, part) = refs[:-4], refs[-4:]
    gates = jnp.concatenate([ref[...] for ref in arrived], axis=0)
    moments = gated(weight, table, gates, late)
    first, second, third = [partial[i] + moment for i, moment in enumerate(moments)]
    spread(first, second, third, own[0:rows].astype(F32), ratio, rel, own_sum, part)


def called(ratio, rel, own_sum, theirs, inverse, finish):
    rows, cols = ratio.shape
    share = 0.5 / (cols * lax.axis_size("tgt"))
    root_half = math.sqrt(0.5 * math.log2(math.e))
    for begin in range(0, rows, LANE):
        row = jnp.broadcast_to(theirs[:, begin : begin + LANE], (LANE, LANE))
        column = jnp.sum(jnp.where(diagonal(), row, 0.0), axis=1, keepdims=True)
        shared = (own_sum[begin : begin + LANE] + column) * share
        for start in range(0, LANE, CHUNK):
            here = slice(begin + start, begin + start + CHUNK)
            spot = shared[start : start + CHUNK]
            by_ploidy = inverse[here]
            centres = [max(state, 0.1) * by_ploidy for state in range(6)]
            widths = [jnp.maximum(centre, 0.25) for centre in centres]
            centres = [centre * root_half for centre in centres]
            for lane in range(0, cols, LANE):
                there = slice(lane, lane + LANE)
                level = 0.5 * rel[here, there] + spot
                copies = ratio[here, there] * root_half
                scores, roots = [], []
                for prior, centre, width in zip(LOG_PRIOR, centres, widths):
                    root = lax.rsqrt(level * width + 0.01)
                    delta = (copies - centre) * root
                    scores.append(prior * math.log2(math.e) - delta * delta)
                    roots.append(root)
                peak = functools.reduce(jnp.maximum, scores)
                expo = [jnp.exp2(s - peak) * root for s, root in zip(scores, roots)]
                tail = top = expo[5]
                for state in range(4, 0, -1):
                    tail = tail + expo[state]
                    top = top + tail
                finish(here, there, top / (tail + expo[0]))


def gate_kernel(asked, ratio, rel, own_sum, theirs, inverse, plf, across, *refs):
    rows = ratio.shape[0]
    mates = (len(refs) - 2) // 4
    half = mates + 1
    noted, passed, gate, out = refs[:mates], refs[mates : 2 * mates], refs[2 * mates], refs[2 * mates + 1 :]

    def finish(here, there, value):
        offset = value - plf[here]
        gate[here, there] = (1.0 / (1.0 + 4.0 * (offset * offset))).astype(BF16)

    called(ratio, rel, own_sum, theirs, inverse, finish)
    for p in range(1, 2 * half):
        if p < half:
            source = noted[p - 1]
        elif p == half:
            source = across
        else:
            source = passed[(p ^ half) - 1]
        place = source.shape[0] - asked + p
        out[p - 1][...] = pick(gate, source[place : place + 1], rows // RBLK)


def final_kernel(ratio, rel, own_sum, theirs, inverse, out):
    def finish(here, there, value):
        out[here, there] = value

    called(ratio, rel, own_sum, theirs, inverse, finish)


def body(coverage, neighbours, nbr_weight, ploidy, gc_bin):
    count = lax.axis_size("samp")
    half = count // 2
    mates = range(1, half)
    rows, cols = coverage.shape
    extra = -(-count // 16) * 16
    late = [3] if half > 3 else []
    bins = lax.broadcasted_iota(jnp.int32, (NGC, cols), 0)
    onehot = (bins == gc_bin[None, :]).astype(F32)
    plf = jnp.broadcast_to(ploidy.astype(F32)[:, None], (rows, LANE))
    inverse = 1.0 / plf

    (mine,) = call(stats_kernel, "bin_sums", [((NGC, rows + LANE), F32)], coverage, onehot)
    theirs = swap_tgt(mine)
    (ask,) = call(
        functools.partial(ask_kernel, rows), "choices", [((extra, cols), BF16)], neighbours
    )
    own, wide = call(
        norm_kernel, "normalise",
        [((rows + extra, cols), BF16), ((rows + 2 * extra, cols), BF16)],
        coverage, mine, theirs, onehot, ask,
    )
    across = send(wide, half, count)
    noted = [send(ask if k in late else own, k, count) for k in mates]
    weight, total = call(
        map_kernel, "weight_map", [((rows, count * RBLK), BF16), ((rows, LANE), F32)],
        neighbours, nbr_weight, plf, own, scratch=[pltpu.VMEM((count, rows, RBLK), F32)],
    )
    passed = call(
        functools.partial(pass_kernel, late, extra), "pass_on",
        [(((2 if k in late else 1) * RBLK + extra, cols), BF16) for k in mates],
        total, own, across, *noted,
    )
    passed = [send(block, k, count) for k, block in zip(mates, passed)]
    spreads = [((rows, cols), F32), ((rows, cols), F32), ((rows, LANE), F32), ((1, rows), F32)]
    early = [0] + [k for k in mates if k not in late] + [half]
    table, partial = call(
        functools.partial(early_one_kernel, early, rows), "early_moments_one",
        [((count * RBLK, cols), BF16), ((2, rows, cols), F32)],
        weight, own, across, ask, *noted,
    )
    table, ratio, rel, own_sum, part = call(
        functools.partial(first_kernel, late, rows), "moments_one",
        [((count * RBLK, cols), BF16)] + spreads,
        weight, total, own, table, partial, *passed,
    )
    gate, *gates = call(
        functools.partial(gate_kernel, extra), "gate",
        [((rows, cols), BF16)] + [((RBLK, cols), BF16)] * (count - 1),
        ratio, rel, own_sum, swap_tgt(part), inverse, plf, across, *noted, *passed,
    )
    order = [half + i for i in (0, 2, 1) if i < half] + list(range(half + 3, count))
    order += list(range(half - 1, 0, -1))
    gates = [send(gates[p - 1], p, count) for p in order]
    last = 1
    (partial,) = call(
        functools.partial(early_two_kernel, order[:-last]), "early_moments_two",
        [((3, rows, cols), F32)], weight, table, gate, ask, *gates[:-last],
    )
    ratio, rel, own_sum, part = call(
        functools.partial(second_kernel, order[-last:], rows), "moments_two", spreads,
        weight, table, own, partial, *gates[-last:],
    )
    (out,) = call(
        final_kernel, "copy_number", [((rows, cols), F32)],
        ratio, rel, own_sum, swap_tgt(part), inverse,
    )
    return out


def solution(mesh):
    in_specs = (
        P("samp", ("slab", "tgt")),
        P("samp", None),
        P("samp", None),
        P("samp"),
        P(("slab", "tgt")),
    )
    out_specs = P("samp", ("slab", "tgt"))
    return jax.shard_map(body, mesh=mesh, in_specs=in_specs, out_specs=out_specs, check_vma=False)
```

```python
import functools
import math

import jax
import jax.numpy as jnp
from jax import lax
from jax.experimental import pallas as pl
from jax.experimental.pallas import tpu as pltpu
from jax.sharding import PartitionSpec as P

NGC = 8
RBLK = 128
LANE = 128
CHUNK = 16
GROUP = 8

LOG_PRIOR = (-4.6051702, -3.2188758, -0.1625189, -2.8134107, -3.5065579, -4.6051702)

F32 = jnp.float32
BF16 = jnp.bfloat16
EXACT = lax.Precision.HIGHEST


def swap_tgt(value):
    return lax.ppermute(value, "tgt", [(0, 1), (1, 0)])


def send(value, step, count):
    return lax.ppermute(value, "samp", [(i, i ^ step) for i in range(count)])


def across_of(half):
    return half + half // 2


def call(body, name, outs, *args, scratch=(), cost=1):
    return pl.pallas_call(
        body,
        out_shape=[jax.ShapeDtypeStruct(shape, dtype) for shape, dtype in outs],
        in_specs=[pl.BlockSpec(memory_space=pltpu.VMEM)] * len(args),
        out_specs=[pl.BlockSpec(memory_space=pltpu.VMEM)] * len(outs),
        scratch_shapes=list(scratch),
        compiler_params=pltpu.CompilerParams(vmem_limit_bytes=16 * 2**20),
        cost_estimate=pl.CostEstimate(flops=cost, bytes_accessed=cost, transcendentals=0),
        name=name,
    )(*args)


def dot(left, right, left_dim, right_dim, precision=None):
    return lax.dot_general(
        left,
        right,
        (((left_dim,), (right_dim,)), ((), ())),
        precision=precision,
        preferred_element_type=F32,
    )


def pick(ref, ask, parts):
    chosen = ref[0:RBLK]
    for part in range(1, parts):
        chosen = jnp.where(ask == part, ref[part * RBLK : (part + 1) * RBLK], chosen)
    return chosen


def ask_kernel(rows, neighbours, ask):
    index = neighbours[...]
    position = lax.div(index, rows) ^ lax.axis_index("samp")
    block = lax.div(lax.rem(index, rows), RBLK)
    count = lax.axis_size("samp")
    best = [
        jnp.max(jnp.where(position == p, block, 0), axis=0, keepdims=True) for p in range(count)
    ]
    best += [jnp.zeros_like(best[0])] * (ask.shape[0] - count)
    best = jnp.max(jnp.concatenate(best, axis=0), axis=1, keepdims=True)
    ask[...] = jnp.broadcast_to(best.astype(F32), ask.shape).astype(BF16)


def map_kernel(neighbours, weight, plf, noted, out, total, inverse, wide):
    rows = neighbours.shape[0]
    listed = neighbours.shape[1]
    count = lax.axis_size("samp")
    me = lax.axis_index("samp")
    sample = lax.broadcasted_iota(jnp.int32, (RBLK, listed), 0).astype(F32).astype(BF16)
    device = lax.broadcasted_iota(jnp.int32, (count, listed), 0)
    one, zero = jnp.ones((), BF16), jnp.zeros((), BF16)

    def step(i, carry):
        start = pl.multiple_of(i * GROUP, GROUP)
        index = neighbours[pl.ds(start, GROUP), :]
        heavy = weight[pl.ds(start, GROUP), :].astype(F32)
        position = lax.div(index, rows) ^ me
        low = lax.rem(index, RBLK).astype(F32).astype(BF16)
        for r in range(0, GROUP, 2):
            low_one = jnp.concatenate(
                [jnp.where(sample == low[q : q + 1], one, zero) for q in (r, r + 1)], axis=1
            )
            high = [
                jnp.where(device == position[q : q + 1], heavy[q : q + 1], 0.0) for q in (r, r + 1)
            ]
            none = jnp.zeros_like(high[0])
            high_one = jnp.concatenate(
                [jnp.concatenate([high[0], none], axis=1), jnp.concatenate([none, high[1]], axis=1)],
                axis=0,
            ).astype(BF16)
            both = dot(high_one, low_one, 1, 1)
            wide[:, pl.ds(start + r, 1), :] = both[:count].reshape(count, 1, RBLK)
            wide[:, pl.ds(start + r + 1, 1), :] = both[count:].reshape(count, 1, RBLK)
        return carry

    lax.fori_loop(0, rows // GROUP, step, 0, unroll=8)
    for p in range(count):
        out[:, p * RBLK : (p + 1) * RBLK] = wide[p].astype(BF16)
    summed = jnp.sum(weight[...].astype(F32), axis=1, keepdims=True)
    total[...] = jnp.broadcast_to(summed, total.shape)
    inverse[...] = 1.0 / plf[...]


def bin_rows(bins):
    return lax.broadcasted_iota(jnp.int32, (NGC, bins.shape[1]), 0) == bins[...]


def stats_kernel(coverage, bins, stats):
    stats[...] = dot(bin_rows(bins).astype(F32).astype(BF16), coverage[...], 1, 1)


def norm_kernel(coverage, mine, theirs, bins, ask, noted, wide):
    rows, cols = coverage.shape[0] - LANE, coverage.shape[1]
    extra = ask.shape[0]
    sums = mine[:, 0:rows] + theirs[:, 0:rows]
    number = mine[:, rows : rows + 1] + theirs[:, rows : rows + 1]
    mean = jnp.sum(sums, axis=0, keepdims=True) / (cols * lax.axis_size("tgt"))
    scale = mean / (sums / jnp.maximum(number, 1.0))
    scale = dot(jnp.where(sums > 0, scale, 0.0), bin_rows(bins).astype(F32), 0, 0, EXACT)
    block = (coverage[0:rows].astype(F32) * scale).astype(BF16)
    for out in (noted, wide):
        out[0:rows] = block
        out[rows : rows + extra] = ask[...]
    wide[rows + extra :] = ask[...]


def pass_kernel(late, asked, total, own, across, *refs):
    mates = len(refs) // 2
    half = mates + 1
    noted, out = refs[:mates], refs[mates:]
    rows = own.shape[0] - asked
    parts = rows // RBLK
    for k in range(1, half):
        note = noted[k - 1]
        base = note.shape[0] - asked
        other = base + (k ^ half)
        out[k - 1][0:RBLK] = pick(across, note[other : other + 1], parts)
        if k in late:
            out[k - 1][RBLK : 2 * RBLK] = pick(own, note[base + k : base + k + 1], parts)


def spread(first, second, third, normf, ratio, rel, own_sum, part):
    inverse = 1.0 / second
    scaled = first * inverse
    ratio[...] = normf * scaled
    relative = (third * inverse) * scaled - 1.0
    rel[...] = relative
    own_sum[...] = jnp.broadcast_to(jnp.sum(relative, axis=1, keepdims=True), own_sum.shape)
    for start in range(0, own_sum.shape[0], LANE):
        block = jnp.where(diagonal(), own_sum[start : start + LANE], 0.0)
        part[:, start : start + LANE] = jnp.sum(block, axis=0, keepdims=True)


def diagonal():
    row = lax.broadcasted_iota(jnp.int32, (LANE, LANE), 0)
    return row == lax.broadcasted_iota(jnp.int32, (LANE, LANE), 1)


def squared(block):
    wide = block.astype(F32)
    return (wide * wide).astype(BF16)


def columns(weight, positions):
    return jnp.concatenate([weight[:, p * RBLK : (p + 1) * RBLK] for p in positions], axis=1)


def place(table, positions):
    return jnp.concatenate([table[p * RBLK : (p + 1) * RBLK] for p in positions], axis=0)


def early_one_kernel(early, rows, weight, own, across, ask, *refs):
    noted, (table, partial) = refs[:-2], refs[-2:]
    parts = rows // RBLK
    half = len(noted) + 1
    for p in early:
        source = own if p == 0 else across if p == half else noted[p - 1]
        table[p * RBLK : (p + 1) * RBLK] = pick(source, ask[p : p + 1], parts)
    mine, block = columns(weight, early), place(table, early)
    partial[0] = dot(mine, block, 1, 0)
    partial[1] = dot(mine, squared(block), 1, 0)


def first_kernel(late, rows, weight, total, own, early, partial, *refs):
    mates = len(refs) - 5
    half = mates + 1
    passed, (table, ratio, rel, own_sum, part) = refs[:mates], refs[mates:]
    cols = own.shape[1]
    table[...] = early[...]
    arrived = []
    for k in range(1, half):
        if k in late:
            arrived.append(k)
            table[k * RBLK : (k + 1) * RBLK] = passed[k - 1][RBLK : 2 * RBLK]
        other = k ^ half
        arrived.append(other)
        table[other * RBLK : (other + 1) * RBLK] = passed[k - 1][0:RBLK]
    mine, block = columns(weight, arrived), place(table, arrived)
    second = partial[0] + dot(mine, block, 1, 0)
    third = partial[1] + dot(mine, squared(block), 1, 0)
    first = jnp.concatenate([total[...]] * (cols // LANE), axis=1)
    spread(first, second, third, own[0:rows].astype(F32), ratio, rel, own_sum, part)


def gated(weight, table, gates, positions):
    mine, block = columns(weight, positions), place(table, positions)
    wide = gates.astype(F32)
    covs = (wide * block.astype(F32)).astype(BF16)
    squares = (wide * squared(block).astype(F32)).astype(BF16)
    return [dot(mine, values, 1, 0) for values in (gates, covs, squares)]


def early_two_kernel(early, weight, table, gate, across, ask, *refs):
    arrived, partial = refs[:-1], refs[-1]
    parts = gate.shape[0] // RBLK
    far = early[-1]
    gates = [pick(gate, ask[0:1], parts)] + [ref[...] for ref in arrived]
    gates = jnp.concatenate(gates + [pick(across, ask[far : far + 1], parts)], axis=0)
    for i, moment in enumerate(gated(weight, table, gates, early)):
        partial[i] = moment


def second_kernel(late, rows, weight, table, own, partial, *refs):
    arrived, (ratio, rel, own_sum, part) = refs[:-4], refs[-4:]
    gates = jnp.concatenate([ref[...] for ref in arrived], axis=0)
    moments = gated(weight, table, gates, late)
    first, second, third = [partial[i] + moment for i, moment in enumerate(moments)]
    spread(first, second, third, own[0:rows].astype(F32), ratio, rel, own_sum, part)


def called(ratio, rel, own_sum, theirs, inverse, finish):
    rows, cols = ratio.shape
    share = 0.5 / (cols * lax.axis_size("tgt"))
    root_half = math.sqrt(0.5 * math.log2(math.e))
    for begin in range(0, rows, LANE):
        row = jnp.broadcast_to(theirs[:, begin : begin + LANE], (LANE, LANE))
        column = jnp.sum(jnp.where(diagonal(), row, 0.0), axis=1, keepdims=True)
        shared = (own_sum[begin : begin + LANE] + column) * share
        for start in range(0, LANE, CHUNK):
            here = slice(begin + start, begin + start + CHUNK)
            spot = shared[start : start + CHUNK]
            by_ploidy = inverse[here]
            centres = [max(state, 0.1) * by_ploidy for state in range(6)]
            widths = [jnp.maximum(centre, 0.25) for centre in centres]
            centres = [centre * root_half for centre in centres]
            for lane in range(0, cols, LANE):
                there = slice(lane, lane + LANE)
                level = 0.5 * rel[here, there] + spot
                copies = ratio[here, there] * root_half
                scores, roots = [], []
                for prior, centre, width in zip(LOG_PRIOR, centres, widths):
                    root = lax.rsqrt(level * width + 0.01)
                    delta = (copies - centre) * root
                    scores.append(prior * math.log2(math.e) - delta * delta)
                    roots.append(root)
                peak = functools.reduce(jnp.maximum, scores)
                expo = [jnp.exp2(s - peak) * root for s, root in zip(scores, roots)]
                tail = top = expo[5]
                for state in range(4, 0, -1):
                    tail = tail + expo[state]
                    top = top + tail
                finish(here, there, top / (tail + expo[0]))


def gate_kernel(order, asked, ratio, rel, own_sum, theirs, inverse, plf, *refs):
    rows = ratio.shape[0]
    noted, gate, out = refs[: len(order)], refs[len(order)], refs[len(order) + 1 :]

    def finish(here, there, value):
        offset = value - plf[here]
        gate[here, there] = (1.0 / (1.0 + 4.0 * (offset * offset))).astype(BF16)

    called(ratio, rel, own_sum, theirs, inverse, finish)
    for k, ref in zip(order, out):
        spot = noted[k - 1].shape[0] - asked + k
        ref[...] = pick(gate, noted[k - 1][spot : spot + 1], rows // RBLK)


def pass_gate_kernel(order, asked, across, *refs):
    noted, out = refs[: len(order)], refs[len(order) :]
    far = across_of(len(order) + 1)
    for k, ref in zip(order, out):
        spot = noted[k - 1].shape[0] - asked + (k ^ far)
        ref[...] = pick(across, noted[k - 1][spot : spot + 1], across.shape[0] // RBLK)


def final_kernel(ratio, rel, own_sum, theirs, inverse, out):
    def finish(here, there, value):
        out[here, there] = value

    called(ratio, rel, own_sum, theirs, inverse, finish)


def body(coverage, neighbours, nbr_weight, ploidy, gc_bin):
    count = lax.axis_size("samp")
    half = count // 2
    mates = range(1, half)
    rows, cols = coverage.shape
    extra = -(-count // 16) * 16
    late = [3] if half > 3 else []
    bins = gc_bin.reshape(1, cols)
    counted = jnp.pad(coverage, ((0, LANE), (0, 0)), constant_values=1)
    plf = jnp.broadcast_to(ploidy.astype(F32)[:, None], (rows, LANE))

    (mine,) = call(stats_kernel, "bin_sums", [((NGC, rows + LANE), F32)], counted, bins)
    theirs = swap_tgt(mine)
    (ask,) = call(
        functools.partial(ask_kernel, rows), "choices", [((extra, cols), BF16)], neighbours
    )
    own, wide = call(
        norm_kernel, "normalise",
        [((rows + extra, cols), BF16), ((rows + 2 * extra, cols), BF16)],
        counted, mine, theirs, bins, ask,
    )
    across = send(wide, half, count)
    noted = [send(ask if k in late else own, k, count) for k in mates]
    weight, total, inverse = call(
        map_kernel, "weight_map",
        [((rows, count * RBLK), BF16), ((rows, LANE), F32), ((rows, LANE), F32)],
        neighbours, nbr_weight, plf, own, scratch=[pltpu.VMEM((count, rows, RBLK), F32)],
    )
    passed = call(
        functools.partial(pass_kernel, late, extra), "pass_on",
        [(((2 if k in late else 1) * RBLK, cols), BF16) for k in mates],
        total, own, across, *noted,
    )
    passed = [send(block, k, count) for k, block in zip(mates, passed)]
    spreads = [((rows, cols), F32), ((rows, cols), F32), ((rows, LANE), F32), ((1, rows), F32)]
    early = [0] + [k for k in mates if k not in late] + [half]
    table, partial = call(
        functools.partial(early_one_kernel, early, rows), "early_moments_one",
        [((count * RBLK, cols), BF16), ((2, rows, cols), F32)],
        weight, own, across, ask, *noted,
    )
    table, ratio, rel, own_sum, part = call(
        functools.partial(first_kernel, late, rows), "moments_one",
        [((count * RBLK, cols), BF16)] + spreads,
        weight, total, own, table, partial, *passed,
    )
    order = list(range(half - 1, 0, -1))
    gate, *gates = call(
        functools.partial(gate_kernel, order, extra), "gate",
        [((rows, cols), BF16)] + [((RBLK, cols), BF16)] * len(order),
        ratio, rel, own_sum, swap_tgt(part), inverse, plf, *noted,
    )
    far = across_of(half)
    far_gate = send(gate, far, count)
    gates = [send(block, k, count) for k, block in zip(order, gates)]
    (partial,) = call(
        functools.partial(early_two_kernel, [0] + order + [far]), "early_moments_two",
        [((3, rows, cols), F32)], weight, table, gate, far_gate, ask, *gates,
    )
    order = [3, 1, 2] if half == 4 else order
    gates = call(
        functools.partial(pass_gate_kernel, order, extra), "pass_on_gate",
        [((RBLK, cols), BF16)] * len(order), far_gate, *noted,
    )
    gates = [send(block, k, count) for k, block in zip(order, gates)]
    ratio, rel, own_sum, part = call(
        functools.partial(second_kernel, [k ^ far for k in order], rows), "moments_two", spreads,
        weight, table, own, partial, *gates,
    )
    (out,) = call(
        final_kernel, "copy_number", [((rows, cols), F32)],
        ratio, rel, own_sum, swap_tgt(part), inverse,
    )
    return out


def solution(mesh):
    in_specs = (
        P("samp", ("slab", "tgt")),
        P("samp", None),
        P("samp", None),
        P("samp"),
        P(("slab", "tgt")),
    )
    out_specs = P("samp", ("slab", "tgt"))
    return jax.shard_map(body, mesh=mesh, in_specs=in_specs, out_specs=out_specs, check_vma=False)
```

```python
import functools
import math

import jax
import jax.numpy as jnp
from jax import lax
from jax.experimental import pallas as pl
from jax.experimental.pallas import tpu as pltpu
from jax.sharding import PartitionSpec as P

NGC = 8
RBLK = 128
LANE = 128
CHUNK = 16
GROUP = 8

LOG_PRIOR = (-4.6051702, -3.2188758, -0.1625189, -2.8134107, -3.5065579, -4.6051702)

F32 = jnp.float32
BF16 = jnp.bfloat16


def swap_tgt(value):
    return lax.ppermute(value, "tgt", [(0, 1), (1, 0)])


def send(value, step, count):
    return lax.ppermute(value, "samp", [(i, i ^ step) for i in range(count)])


def across_of(half):
    return half + half // 2


def call(body, name, outs, *args, scratch=(), cost=1):
    return pl.pallas_call(
        body,
        out_shape=[jax.ShapeDtypeStruct(shape, dtype) for shape, dtype in outs],
        in_specs=[pl.BlockSpec(memory_space=pltpu.VMEM)] * len(args),
        out_specs=[pl.BlockSpec(memory_space=pltpu.VMEM)] * len(outs),
        scratch_shapes=list(scratch),
        compiler_params=pltpu.CompilerParams(vmem_limit_bytes=16 * 2**20),
        cost_estimate=pl.CostEstimate(flops=cost, bytes_accessed=cost, transcendentals=0),
        name=name,
    )(*args)


def dot(left, right, left_dim, right_dim):
    dims = (((left_dim,), (right_dim,)), ((), ()))
    return lax.dot_general(left, right, dims, preferred_element_type=F32)


def pick(ref, ask, parts):
    chosen = ref[0:RBLK]
    for part in range(1, parts):
        chosen = jnp.where(ask == part, ref[part * RBLK : (part + 1) * RBLK], chosen)
    return chosen


def ask_kernel(rows, neighbours, ask):
    index = neighbours[...]
    position = lax.div(index, rows) ^ lax.axis_index("samp")
    block = lax.div(lax.rem(index, rows), RBLK)
    count = lax.axis_size("samp")
    best = [
        jnp.max(jnp.where(position == p, block, 0), axis=0, keepdims=True) for p in range(count)
    ]
    best += [jnp.zeros_like(best[0])] * (ask.shape[0] - count)
    best = jnp.max(jnp.concatenate(best, axis=0), axis=1, keepdims=True)
    ask[...] = jnp.broadcast_to(best.astype(F32), ask.shape).astype(BF16)


def map_kernel(neighbours, weight, plf, noted, out, total, inverse, wide):
    rows = neighbours.shape[0]
    listed = neighbours.shape[1]
    count = lax.axis_size("samp")
    me = lax.axis_index("samp")
    sample = lax.broadcasted_iota(jnp.int32, (RBLK, listed), 0).astype(F32).astype(BF16)
    device = lax.broadcasted_iota(jnp.int32, (count, listed), 0)
    one, zero = jnp.ones((), BF16), jnp.zeros((), BF16)

    def step(i, carry):
        start = pl.multiple_of(i * GROUP, GROUP)
        index = neighbours[pl.ds(start, GROUP), :]
        heavy = weight[pl.ds(start, GROUP), :].astype(F32)
        position = lax.div(index, rows) ^ me
        low = lax.rem(index, RBLK).astype(F32).astype(BF16)
        for r in range(0, GROUP, 2):
            low_one = jnp.concatenate(
                [jnp.where(sample == low[q : q + 1], one, zero) for q in (r, r + 1)], axis=1
            )
            high = [
                jnp.where(device == position[q : q + 1], heavy[q : q + 1], 0.0) for q in (r, r + 1)
            ]
            none = jnp.zeros_like(high[0])
            high_one = jnp.concatenate(
                [jnp.concatenate([high[0], none], axis=1), jnp.concatenate([none, high[1]], axis=1)],
                axis=0,
            ).astype(BF16)
            both = dot(high_one, low_one, 1, 1)
            wide[:, pl.ds(start + r, 1), :] = both[:count].reshape(count, 1, RBLK)
            wide[:, pl.ds(start + r + 1, 1), :] = both[count:].reshape(count, 1, RBLK)
        return carry

    lax.fori_loop(0, rows // GROUP, step, 0, unroll=8)
    for p in range(count):
        out[:, p * RBLK : (p + 1) * RBLK] = wide[p].astype(BF16)
    summed = jnp.sum(weight[...].astype(F32), axis=1, keepdims=True)
    total[...] = jnp.broadcast_to(summed, total.shape)
    inverse[...] = 1.0 / plf[...]


def bin_rows(bins):
    return lax.broadcasted_iota(jnp.int32, (NGC, bins.shape[1]), 0) == bins[...]


def stats_kernel(coverage, bins, stats):
    stats[...] = dot(bin_rows(bins).astype(F32).astype(BF16), coverage[...], 1, 1)


def spread_bins(scale, bins):
    terms = []
    for _ in range(3):
        terms.append(scale.astype(BF16).astype(F32))
        scale = scale - terms[-1]
    picked = bin_rows(bins).astype(F32)
    left = jnp.concatenate(terms, axis=0).astype(BF16)
    return dot(left, jnp.concatenate([picked] * 3, axis=0).astype(BF16), 0, 0)


def norm_kernel(coverage, mine, theirs, bins, ask, noted, plain):
    rows, cols = coverage.shape[0] - LANE, coverage.shape[1]
    extra = ask.shape[0]
    sums = mine[:, 0:rows] + theirs[:, 0:rows]
    number = mine[:, rows : rows + 1] + theirs[:, rows : rows + 1]
    mean = jnp.sum(sums, axis=0, keepdims=True) / (cols * lax.axis_size("tgt"))
    scale = mean / (sums / jnp.maximum(number, 1.0))
    scale = spread_bins(jnp.where(sums > 0, scale, 0.0), bins)
    block = (coverage[0:rows].astype(F32) * scale).astype(BF16)
    plain[...] = block
    noted[0:rows] = block
    noted[rows : rows + extra] = ask[...]


def pass_kernel(late, asked, total, own, across, *refs):
    mates = len(refs) // 2
    half = mates + 1
    noted, out = refs[:mates], refs[mates:]
    rows = own.shape[0] - asked
    parts = rows // RBLK
    for k in range(1, half):
        note = noted[k - 1]
        base = note.shape[0] - asked
        other = base + (k ^ half)
        out[k - 1][0:RBLK] = pick(across, note[other : other + 1], parts)
        if k in late:
            out[k - 1][RBLK : 2 * RBLK] = pick(own, note[base + k : base + k + 1], parts)


def spread(first, second, third, normf, ratio, rel, own_sum, part):
    inverse = 1.0 / second
    scaled = first * inverse
    ratio[...] = normf * scaled
    relative = (third * inverse) * scaled - 1.0
    rel[...] = relative
    own_sum[...] = jnp.broadcast_to(jnp.sum(relative, axis=1, keepdims=True), own_sum.shape)
    for start in range(0, own_sum.shape[0], LANE):
        block = jnp.where(diagonal(), own_sum[start : start + LANE], 0.0)
        part[:, start : start + LANE] = jnp.sum(block, axis=0, keepdims=True)


def diagonal():
    row = lax.broadcasted_iota(jnp.int32, (LANE, LANE), 0)
    return row == lax.broadcasted_iota(jnp.int32, (LANE, LANE), 1)


def squared(block):
    wide = block.astype(F32)
    return (wide * wide).astype(BF16)


def columns(weight, positions):
    return jnp.concatenate([weight[:, p * RBLK : (p + 1) * RBLK] for p in positions], axis=1)


def place(table, positions):
    return jnp.concatenate([table[p * RBLK : (p + 1) * RBLK] for p in positions], axis=0)


def early_one_kernel(early, rows, weight, own, across, ask, *refs):
    noted, (table, partial) = refs[:-2], refs[-2:]
    parts = rows // RBLK
    half = len(noted) + 1
    for p in early:
        source = own if p == 0 else across if p == half else noted[p - 1]
        table[p * RBLK : (p + 1) * RBLK] = pick(source, ask[p : p + 1], parts)
    mine, block = columns(weight, early), place(table, early)
    partial[0] = dot(mine, block, 1, 0)
    partial[1] = dot(mine, squared(block), 1, 0)


def first_kernel(late, rows, weight, total, own, early, partial, *refs):
    mates = len(refs) - 5
    half = mates + 1
    passed, (table, ratio, rel, own_sum, part) = refs[:mates][::-1], refs[mates:]
    cols = own.shape[1]
    table[...] = early[...]
    arrived = []
    for k in range(1, half):
        if k in late:
            arrived.append(k)
            table[k * RBLK : (k + 1) * RBLK] = passed[k - 1][RBLK : 2 * RBLK]
        other = k ^ half
        arrived.append(other)
        table[other * RBLK : (other + 1) * RBLK] = passed[k - 1][0:RBLK]
    mine, block = columns(weight, arrived), place(table, arrived)
    second = partial[0] + dot(mine, block, 1, 0)
    third = partial[1] + dot(mine, squared(block), 1, 0)
    first = jnp.concatenate([total[...]] * (cols // LANE), axis=1)
    spread(first, second, third, own[0:rows].astype(F32), ratio, rel, own_sum, part)


def gated(weight, table, gates, positions):
    mine, block = columns(weight, positions), place(table, positions)
    wide = gates.astype(F32)
    covs = (wide * block.astype(F32)).astype(BF16)
    squares = (wide * squared(block).astype(F32)).astype(BF16)
    return [dot(mine, values, 1, 0) for values in (gates, covs, squares)]


def early_two_kernel(early, weight, table, gate, across, ask, *refs):
    arrived, partial = refs[:-1], refs[-1]
    parts = gate.shape[0] // RBLK
    far = early[-1]
    gates = [pick(gate, ask[0:1], parts)] + [ref[...] for ref in arrived]
    gates = jnp.concatenate(gates + [pick(across, ask[far : far + 1], parts)], axis=0)
    for i, moment in enumerate(gated(weight, table, gates, early)):
        partial[i] = moment


def second_kernel(late, rows, weight, table, own, partial, *refs):
    arrived, (ratio, rel, own_sum, part) = refs[:-4], refs[-4:]
    gates = jnp.concatenate([ref[...] for ref in arrived], axis=0)
    moments = gated(weight, table, gates, late)
    first, second, third = [partial[i] + moment for i, moment in enumerate(moments)]
    spread(first, second, third, own[0:rows].astype(F32), ratio, rel, own_sum, part)


def called(ratio, rel, own_sum, theirs, inverse, finish):
    rows, cols = ratio.shape
    share = 0.5 / (cols * lax.axis_size("tgt"))
    root_half = math.sqrt(0.5 * math.log2(math.e))
    for begin in range(0, rows, LANE):
        row = jnp.broadcast_to(theirs[:, begin : begin + LANE], (LANE, LANE))
        column = jnp.sum(jnp.where(diagonal(), row, 0.0), axis=1, keepdims=True)
        shared = (own_sum[begin : begin + LANE] + column) * share
        for start in range(0, LANE, CHUNK):
            here = slice(begin + start, begin + start + CHUNK)
            spot = shared[start : start + CHUNK]
            by_ploidy = inverse[here]
            centres = [max(state, 0.1) * by_ploidy for state in range(6)]
            widths = [jnp.maximum(centre, 0.25) for centre in centres]
            centres = [centre * root_half for centre in centres]
            for lane in range(0, cols, LANE):
                there = slice(lane, lane + LANE)
                level = 0.5 * rel[here, there] + spot
                copies = ratio[here, there] * root_half
                scores, roots = [], []
                for prior, centre, width in zip(LOG_PRIOR, centres, widths):
                    root = lax.rsqrt(level * width + 0.01)
                    delta = (copies - centre) * root
                    scores.append(prior * math.log2(math.e) - delta * delta)
                    roots.append(root)
                peak = functools.reduce(jnp.maximum, scores)
                expo = [jnp.exp2(s - peak) * root for s, root in zip(scores, roots)]
                tail = top = expo[5]
                for state in range(4, 0, -1):
                    tail = tail + expo[state]
                    top = top + tail
                finish(here, there, top / (tail + expo[0]))


def gate_kernel(order, asked, ratio, rel, own_sum, theirs, inverse, plf, *refs):
    rows = ratio.shape[0]
    noted, gate, out = refs[: len(order)], refs[len(order)], refs[len(order) + 1 :]

    def finish(here, there, value):
        offset = value - plf[here]
        gate[here, there] = (1.0 / (1.0 + 4.0 * (offset * offset))).astype(BF16)

    called(ratio, rel, own_sum, theirs, inverse, finish)
    for k, ref in zip(order, out):
        spot = noted[k - 1].shape[0] - asked + k
        ref[...] = pick(gate, noted[k - 1][spot : spot + 1], rows // RBLK)


def pass_gate_kernel(order, asked, across, *refs):
    noted, out = refs[: len(order)], refs[len(order) :]
    far = across_of(len(order) + 1)
    for k, ref in zip(order, out):
        spot = noted[k - 1].shape[0] - asked + (k ^ far)
        ref[...] = pick(across, noted[k - 1][spot : spot + 1], across.shape[0] // RBLK)


def final_kernel(ratio, rel, own_sum, theirs, inverse, out):
    def finish(here, there, value):
        out[here, there] = value

    called(ratio, rel, own_sum, theirs, inverse, finish)


def body(coverage, neighbours, nbr_weight, ploidy, gc_bin):
    count = lax.axis_size("samp")
    half = count // 2
    mates = range(1, half)
    rows, cols = coverage.shape
    extra = -(-count // 16) * 16
    late = [3] if half > 3 else []
    bins = gc_bin.reshape(1, cols)
    counted = jnp.pad(coverage, ((0, LANE), (0, 0)), constant_values=1)
    plf = jnp.broadcast_to(ploidy.astype(F32)[:, None], (rows, LANE))

    (mine,) = call(stats_kernel, "bin_sums", [((NGC, rows + LANE), F32)], counted, bins)
    theirs = swap_tgt(mine)
    (ask,) = call(
        functools.partial(ask_kernel, rows), "choices", [((extra, cols), BF16)], neighbours
    )
    own, plain = call(
        norm_kernel, "normalise",
        [((rows + extra, cols), BF16), ((rows, cols), BF16)],
        counted, mine, theirs, bins, ask,
    )
    across = send(plain, half, count)
    noted = [send(ask if k in late else own, k, count) for k in mates]
    weight, total, inverse = call(
        map_kernel, "weight_map",
        [((rows, count * RBLK), BF16), ((rows, LANE), F32), ((rows, LANE), F32)],
        neighbours, nbr_weight, plf, own, scratch=[pltpu.VMEM((count, rows, RBLK), F32)],
    )
    passed = call(
        functools.partial(pass_kernel, late, extra), "pass_on",
        [(((2 if k in late else 1) * RBLK, cols), BF16) for k in mates],
        total, own, across, *noted,
    )
    passed = [send(block, k, count) for k, block in zip(mates, passed)]
    spreads = [((rows, cols), F32), ((rows, cols), F32), ((rows, LANE), F32), ((1, rows), F32)]
    early = [0] + [k for k in mates if k not in late] + [half]
    table, partial = call(
        functools.partial(early_one_kernel, early, rows), "early_moments_one",
        [((count * RBLK, cols), BF16), ((2, rows, cols), F32)],
        weight, own, across, ask, *noted,
    )
    table, ratio, rel, own_sum, part = call(
        functools.partial(first_kernel, late, rows), "moments_one",
        [((count * RBLK, cols), BF16)] + spreads,
        weight, total, own, table, partial, *passed[::-1],
    )
    order = list(range(half - 1, 0, -1))
    gate, *gates = call(
        functools.partial(gate_kernel, order, extra), "gate",
        [((rows, cols), BF16)] + [((RBLK, cols), BF16)] * len(order),
        ratio, rel, own_sum, swap_tgt(part), inverse, plf, *noted,
    )
    far = across_of(half)
    far_gate = send(gate, far, count)
    gates = [send(block, k, count) for k, block in zip(order, gates)]
    (partial,) = call(
        functools.partial(early_two_kernel, [0] + order + [far]), "early_moments_two",
        [((3, rows, cols), F32)], weight, table, gate, far_gate, ask, *gates,
    )
    order = [3, 1, 2] if half == 4 else order
    gates = call(
        functools.partial(pass_gate_kernel, order, extra), "pass_on_gate",
        [((RBLK, cols), BF16)] * len(order), far_gate, *noted,
    )
    gates = [send(block, k, count) for k, block in zip(order, gates)]
    ratio, rel, own_sum, part = call(
        functools.partial(second_kernel, [k ^ far for k in order], rows), "moments_two", spreads,
        weight, table, own, partial, *gates,
    )
    (out,) = call(
        final_kernel, "copy_number", [((rows, cols), F32)],
        ratio, rel, own_sum, swap_tgt(part), inverse,
    )
    return out


def solution(mesh):
    in_specs = (
        P("samp", ("slab", "tgt")),
        P("samp", None),
        P("samp", None),
        P("samp"),
        P(("slab", "tgt")),
    )
    out_specs = P("samp", ("slab", "tgt"))
    return jax.shard_map(body, mesh=mesh, in_specs=in_specs, out_specs=out_specs, check_vma=False)
```

```python
import functools
import math

import jax
import jax.numpy as jnp
from jax import lax
from jax.experimental import pallas as pl
from jax.experimental.pallas import tpu as pltpu
from jax.sharding import PartitionSpec as P

NGC = 8
RBLK = 128
LANE = 128
CHUNK = 16
GROUP = 16

LOG_PRIOR = (-4.6051702, -3.2188758, -0.1625189, -2.8134107, -3.5065579, -4.6051702)

F32 = jnp.float32
BF16 = jnp.bfloat16


def swap_tgt(value):
    return lax.ppermute(value, "tgt", [(0, 1), (1, 0)])


def send(value, step, count):
    return lax.ppermute(value, "samp", [(i, i ^ step) for i in range(count)])


BLOCK_ACROSS, GATE_ACROSS = 4, 6
NOTED, PASSED, OWN_GATES, PASSED_GATES = (1, 2, 3), (3, 2, 1), (3, 2, 1), (3, 1, 2)
SPARE = 0


def order_of(given, half):
    return list(given) if half == 4 else list(range(1, half))


def block_across(half):
    return BLOCK_ACROSS if half == 4 else half


def gate_across(half):
    return GATE_ACROSS if half == 4 else half


def call(body, name, outs, *args, scratch=(), cost=1):
    return pl.pallas_call(
        body,
        out_shape=[jax.ShapeDtypeStruct(shape, dtype) for shape, dtype in outs],
        in_specs=[pl.BlockSpec(memory_space=pltpu.VMEM)] * len(args),
        out_specs=[pl.BlockSpec(memory_space=pltpu.VMEM)] * len(outs),
        scratch_shapes=list(scratch),
        compiler_params=pltpu.CompilerParams(vmem_limit_bytes=16 * 2**20),
        cost_estimate=pl.CostEstimate(flops=cost, bytes_accessed=cost, transcendentals=0),
        name=name,
    )(*args)


def dot(left, right, left_dim, right_dim):
    dims = (((left_dim,), (right_dim,)), ((), ()))
    return lax.dot_general(left, right, dims, preferred_element_type=F32)


def line(ref, at):
    start = at // 16 * 16
    return ref[start : start + 16][at - start : at - start + 1]


def pick(ref, ask, parts):
    chosen = ref[0:RBLK]
    for part in range(1, parts):
        chosen = jnp.where(ask == part, ref[part * RBLK : (part + 1) * RBLK], chosen)
    return chosen


def ask_kernel(rows, neighbours, ask):
    index = neighbours[...]
    position = lax.div(index, rows) ^ lax.axis_index("samp")
    block = lax.div(lax.rem(index, rows), RBLK)
    count = lax.axis_size("samp")
    best = [
        jnp.max(jnp.where(position == p, block, 0), axis=0, keepdims=True) for p in range(count)
    ]
    best += [jnp.zeros_like(best[0])] * (ask.shape[0] - count)
    best = jnp.max(jnp.concatenate(best, axis=0), axis=1, keepdims=True)
    ask[...] = jnp.broadcast_to(best.astype(F32), ask.shape).astype(BF16)


def map_kernel(neighbours, weight, plf, noted, out, total, inverse, wide):
    rows = neighbours.shape[0]
    listed = neighbours.shape[1]
    count = lax.axis_size("samp")
    me = lax.axis_index("samp")
    sample = lax.broadcasted_iota(jnp.int32, (RBLK, listed), 0).astype(F32).astype(BF16)
    device = lax.broadcasted_iota(jnp.int32, (count, listed), 0)
    one, zero = jnp.ones((), BF16), jnp.zeros((), BF16)

    def step(i, carry):
        start = pl.multiple_of(i * GROUP, GROUP)
        index = neighbours[pl.ds(start, GROUP), :]
        heavy = weight[pl.ds(start, GROUP), :].astype(F32)
        position = lax.div(index, rows) ^ me
        low = lax.rem(index, RBLK).astype(F32).astype(BF16)
        for r in range(0, GROUP, 2):
            low_one = jnp.concatenate(
                [jnp.where(sample == low[q : q + 1], one, zero) for q in (r, r + 1)], axis=1
            )
            high = [
                jnp.where(device == position[q : q + 1], heavy[q : q + 1], 0.0) for q in (r, r + 1)
            ]
            none = jnp.zeros_like(high[0])
            high_one = jnp.concatenate(
                [jnp.concatenate([high[0], none], axis=1), jnp.concatenate([none, high[1]], axis=1)],
                axis=0,
            ).astype(BF16)
            both = dot(high_one, low_one, 1, 1)
            wide[:, pl.ds(start + r, 1), :] = both[:count].reshape(count, 1, RBLK)
            wide[:, pl.ds(start + r + 1, 1), :] = both[count:].reshape(count, 1, RBLK)
        return carry

    lax.fori_loop(0, rows // GROUP, step, 0, unroll=8)
    for p in range(count):
        out[:, p * RBLK : (p + 1) * RBLK] = wide[p].astype(BF16)
    summed = jnp.sum(weight[...].astype(F32), axis=1, keepdims=True)
    total[...] = jnp.broadcast_to(summed, total.shape)
    inverse[...] = 1.0 / plf[...]


def bin_rows(bins):
    return lax.broadcasted_iota(jnp.int32, (NGC, bins.shape[1]), 0) == bins[...]


def stats_kernel(coverage, bins, stats):
    stats[...] = dot(bin_rows(bins).astype(F32).astype(BF16), coverage[...], 1, 1)


def spread_bins(scale, bins):
    terms = []
    for _ in range(3):
        terms.append(scale.astype(BF16).astype(F32))
        scale = scale - terms[-1]
    picked = bin_rows(bins).astype(F32)
    left = jnp.concatenate(terms, axis=0).astype(BF16)
    return dot(left, jnp.concatenate([picked] * 3, axis=0).astype(BF16), 0, 0)


def norm_kernel(coverage, mine, theirs, bins, ask, noted, plain):
    rows, cols = coverage.shape[0] - LANE, coverage.shape[1]
    extra = ask.shape[0]
    sums = mine[:, 0:rows] + theirs[:, 0:rows]
    number = mine[:, rows : rows + 1] + theirs[:, rows : rows + 1]
    mean = jnp.sum(sums, axis=0, keepdims=True) / (cols * lax.axis_size("tgt"))
    scale = mean / (sums / jnp.maximum(number, 1.0))
    scale = spread_bins(jnp.where(sums > 0, scale, 0.0), bins)
    block = (coverage[0:rows].astype(F32) * scale).astype(BF16)
    plain[0:rows] = block
    noted[0:rows] = block
    noted[rows : rows + extra] = ask[...]


def pass_kernel(late, asked, total, own, across, *refs):
    mates = len(refs) // 2
    half = mates + 1
    order, out = order_of(NOTED, half), refs[mates:]
    rows = own.shape[0] - asked
    parts = rows // RBLK
    for k in range(1, half):
        note = refs[order.index(k)]
        base = note.shape[0] - asked
        other = base + (k ^ block_across(half))
        out[k - 1][0:RBLK] = pick(across, line(note, other), parts)
        if k in late:
            out[k - 1][RBLK : 2 * RBLK] = pick(own, line(note, base + k), parts)


def spread(first, second, third, normf, ratio, rel, own_sum, part):
    inverse = 1.0 / second
    scaled = first * inverse
    ratio[...] = normf * scaled
    relative = (third * inverse) * scaled - 1.0
    rel[...] = relative
    own_sum[...] = jnp.broadcast_to(jnp.sum(relative, axis=1, keepdims=True), own_sum.shape)
    for start in range(0, own_sum.shape[0], LANE):
        block = jnp.where(diagonal(), own_sum[start : start + LANE], 0.0)
        part[:, start : start + LANE] = jnp.sum(block, axis=0, keepdims=True)


def diagonal():
    row = lax.broadcasted_iota(jnp.int32, (LANE, LANE), 0)
    return row == lax.broadcasted_iota(jnp.int32, (LANE, LANE), 1)


def squared(block):
    wide = block.astype(F32)
    return (wide * wide).astype(BF16)


def columns(weight, positions):
    return jnp.concatenate([weight[:, p * RBLK : (p + 1) * RBLK] for p in positions], axis=1)


def place(table, positions):
    return jnp.concatenate([table[p * RBLK : (p + 1) * RBLK] for p in positions], axis=0)


def early_one_kernel(early, rows, weight, own, across, ask, *refs):
    noted, (table, partial) = refs[:-2], refs[-2:]
    parts = rows // RBLK
    half = len(noted) + 1
    for p in early:
        source = own if p == 0 else across if p == early[-1] else noted[p - 1]
        table[p * RBLK : (p + 1) * RBLK] = pick(source, line(ask, p), parts)
    mine, block = columns(weight, early), place(table, early)
    partial[0] = dot(mine, block, 1, 0)
    partial[1] = dot(mine, squared(block), 1, 0)


def first_kernel(late, rows, weight, total, own, early, partial, *refs):
    mates = len(refs) - 5
    half = mates + 1
    order, (table, ratio, rel, own_sum, part) = order_of(PASSED, half), refs[mates:]
    cols = own.shape[1]
    table[...] = early[...]
    arrived = []
    for k, ref in zip(order, refs):
        if k in late:
            arrived.append(k)
            table[k * RBLK : (k + 1) * RBLK] = ref[RBLK : 2 * RBLK]
        other = k ^ block_across(half)
        arrived.append(other)
        table[other * RBLK : (other + 1) * RBLK] = ref[0:RBLK]
    mine, block = columns(weight, arrived), place(table, arrived)
    second = partial[0] + dot(mine, block, 1, 0)
    third = partial[1] + dot(mine, squared(block), 1, 0)
    first = jnp.concatenate([total[...]] * (cols // LANE), axis=1)
    spread(first, second, third, own[0:rows].astype(F32), ratio, rel, own_sum, part)


def gated(weight, table, gates, positions):
    mine, block = columns(weight, positions), place(table, positions)
    wide = gates.astype(F32)
    covs = (wide * block.astype(F32)).astype(BF16)
    squares = (wide * squared(block).astype(F32)).astype(BF16)
    return [dot(mine, values, 1, 0) for values in (gates, covs, squares)]


def early_two_kernel(early, weight, table, gate, across, ask, *refs):
    arrived, partial = refs[:-1], refs[-1]
    parts = gate.shape[0] // RBLK
    far = early[-1]
    gates = [pick(gate, line(ask, 0), parts)] + [ref[...] for ref in arrived]
    gates = jnp.concatenate(gates + [pick(across, line(ask, far), parts)], axis=0)
    for i, moment in enumerate(gated(weight, table, gates, early)):
        partial[i] = moment


def second_kernel(late, rows, weight, table, own, partial, *refs):
    arrived, (ratio, rel, own_sum, part) = refs[:-4], refs[-4:]
    gates = jnp.concatenate([ref[...] for ref in arrived], axis=0)
    moments = gated(weight, table, gates, late)
    first, second, third = [partial[i] + moment for i, moment in enumerate(moments)]
    spread(first, second, third, own[0:rows].astype(F32), ratio, rel, own_sum, part)


def called(ratio, rel, own_sum, theirs, inverse, finish):
    rows, cols = ratio.shape
    share = 0.5 / (cols * lax.axis_size("tgt"))
    root_half = math.sqrt(0.5 * math.log2(math.e))
    for begin in range(0, rows, LANE):
        row = jnp.broadcast_to(theirs[:, begin : begin + LANE], (LANE, LANE))
        column = jnp.sum(jnp.where(diagonal(), row, 0.0), axis=1, keepdims=True)
        shared = (own_sum[begin : begin + LANE] + column) * share
        for start in range(0, LANE, CHUNK):
            here = slice(begin + start, begin + start + CHUNK)
            spot = shared[start : start + CHUNK]
            by_ploidy = inverse[here]
            step = by_ploidy * root_half
            for lane in range(0, cols, LANE):
                there = slice(lane, lane + LANE)
                level = 0.5 * rel[here, there] + spot
                copies = ratio[here, there] * root_half
                grow = level * by_ploidy
                scores, roots = [], []
                for state, prior in enumerate(LOG_PRIOR):
                    if state == 0:
                        var, delta = 0.25 * level + 0.01, copies - 0.1 * step
                    elif state == 1:
                        var, delta = grow + 0.01, copies - step
                    else:
                        var, delta = var + grow, delta - step
                    roots.append(lax.rsqrt(var))
                    score = delta * roots[state]
                    scores.append(prior * math.log2(math.e) - score * score)
                peak = functools.reduce(jnp.maximum, scores)
                expo = [jnp.exp2(s - peak) * root for s, root in zip(scores, roots)]
                tail = top = expo[5]
                for state in range(4, 0, -1):
                    tail = tail + expo[state]
                    top = top + tail
                finish(here, there, top / (tail + expo[0]))


def gate_kernel(order, asked, ratio, rel, own_sum, theirs, inverse, plf, *refs):
    rows = ratio.shape[0]
    noted, gate, out = refs[: len(order)], refs[len(order)], refs[len(order) + 1 :]

    def finish(here, there, value):
        offset = value - plf[here]
        gate[here, there] = (1.0 / (1.0 + 4.0 * (offset * offset))).astype(BF16)

    called(ratio, rel, own_sum, theirs, inverse, finish)
    for k, ref in zip(order, out):
        spot = noted[k - 1].shape[0] - asked + k
        ref[...] = pick(gate, line(noted[k - 1], spot), rows // RBLK)


def pass_gate_kernel(order, asked, across, *refs):
    noted, out = refs[: len(order)], refs[len(order) :]
    far = gate_across(len(order) + 1)
    for k, ref in zip(order, out):
        spot = noted[k - 1].shape[0] - asked + (k ^ far)
        ref[...] = pick(across, line(noted[k - 1], spot), across.shape[0] // RBLK)


def final_kernel(ratio, rel, own_sum, theirs, inverse, out):
    def finish(here, there, value):
        out[here, there] = value

    called(ratio, rel, own_sum, theirs, inverse, finish)


def body(coverage, neighbours, nbr_weight, ploidy, gc_bin):
    count = lax.axis_size("samp")
    half = count // 2
    mates = range(1, half)
    rows, cols = coverage.shape
    extra = -(-count // 16) * 16
    late = [3] if half > 3 else []
    bins = gc_bin.reshape(1, cols)
    counted = jnp.pad(coverage, ((0, LANE), (0, 0)), constant_values=1)
    plf = jnp.broadcast_to(ploidy.astype(F32)[:, None], (rows, LANE))

    (mine,) = call(stats_kernel, "bin_sums", [((NGC, rows + LANE), F32)], counted, bins)
    theirs = swap_tgt(mine)
    (ask,) = call(
        functools.partial(ask_kernel, rows), "choices", [((extra, cols), BF16)], neighbours
    )
    own, plain = call(
        norm_kernel, "normalise",
        [((rows + extra, cols), BF16), ((rows + SPARE, cols), BF16)],
        counted, mine, theirs, bins, ask,
    )
    across = send(plain, block_across(half), count)
    noted = [send(ask if k in late else own, k, count) for k in mates]
    weight, total, inverse = call(
        map_kernel, "weight_map",
        [((rows, count * RBLK), BF16), ((rows, LANE), F32), ((rows, LANE), F32)],
        neighbours, nbr_weight, plf, own, scratch=[pltpu.VMEM((count, rows, RBLK), F32)],
    )
    passed = call(
        functools.partial(pass_kernel, late, extra), "pass_on",
        [(((2 if k in late else 1) * RBLK, cols), BF16) for k in mates],
        total, own, across, *[noted[k - 1] for k in order_of(NOTED, half)],
    )
    passed = [send(block, k, count) for k, block in zip(mates, passed)]
    spreads = [((rows, cols), F32), ((rows, cols), F32), ((rows, LANE), F32), ((1, rows), F32)]
    early = [0] + [k for k in mates if k not in late] + [block_across(half)]
    table, partial = call(
        functools.partial(early_one_kernel, early, rows), "early_moments_one",
        [((count * RBLK, cols), BF16), ((2, rows, cols), F32)],
        weight, own, across, ask, *noted,
    )
    table, ratio, rel, own_sum, part = call(
        functools.partial(first_kernel, late, rows), "moments_one",
        [((count * RBLK, cols), BF16)] + spreads,
        weight, total, own, table, partial, *[passed[k - 1] for k in order_of(PASSED, half)],
    )
    order = order_of(OWN_GATES, half)
    gate, *gates = call(
        functools.partial(gate_kernel, order, extra), "gate",
        [((rows, cols), BF16)] + [((RBLK, cols), BF16)] * len(order),
        ratio, rel, own_sum, swap_tgt(part), inverse, plf, *noted,
    )
    far = gate_across(half)
    far_gate = send(gate, far, count)
    gates = [send(block, k, count) for k, block in zip(order, gates)]
    (partial,) = call(
        functools.partial(early_two_kernel, [0] + order + [far]), "early_moments_two",
        [((3, rows, cols), F32)], weight, table, gate, far_gate, ask, *gates,
    )
    order = order_of(PASSED_GATES, half)
    gates = call(
        functools.partial(pass_gate_kernel, order, extra), "pass_on_gate",
        [((RBLK, cols), BF16)] * len(order), far_gate, *noted,
    )
    gates = [send(block, k, count) for k, block in zip(order, gates)]
    ratio, rel, own_sum, part = call(
        functools.partial(second_kernel, [k ^ far for k in order], rows), "moments_two", spreads,
        weight, table, own, partial, *gates,
    )
    (out,) = call(
        final_kernel, "copy_number", [((rows, cols), F32)],
        ratio, rel, own_sum, swap_tgt(part), inverse,
    )
    return out


def solution(mesh):
    in_specs = (
        P("samp", ("slab", "tgt")),
        P("samp", None),
        P("samp", None),
        P("samp"),
        P(("slab", "tgt")),
    )
    out_specs = P("samp", ("slab", "tgt"))
    return jax.shard_map(body, mesh=mesh, in_specs=in_specs, out_specs=out_specs, check_vma=False)
```

```python
import functools
import math

import jax
import jax.numpy as jnp
from jax import lax
from jax.experimental import pallas as pl
from jax.experimental.pallas import tpu as pltpu
from jax.sharding import PartitionSpec as P

NGC = 8
RBLK = 128
LANE = 128
CHUNK = 16
GROUP = 16

LOG_PRIOR = (-4.6051702, -3.2188758, -0.1625189, -2.8134107, -3.5065579, -4.6051702)

F32 = jnp.float32
BF16 = jnp.bfloat16


def swap_tgt(value):
    return lax.ppermute(value, "tgt", [(0, 1), (1, 0)])


def send(value, step, count):
    return lax.ppermute(value, "samp", [(i, i ^ step) for i in range(count)])


BLOCK_ACROSS, GATE_ACROSS = 4, 6
NOTED, PASSED, OWN_GATES, PASSED_GATES = (1, 2, 3), (3, 2, 1), (3, 2, 1), (3, 1, 2)
SPARE = 0


def order_of(given, half):
    return list(given) if half == 4 else list(range(1, half))


def block_across(half):
    return BLOCK_ACROSS if half == 4 else half


def gate_across(half):
    return GATE_ACROSS if half == 4 else half


def call(body, name, outs, *args, scratch=(), cost=1):
    return pl.pallas_call(
        body,
        out_shape=[jax.ShapeDtypeStruct(shape, dtype) for shape, dtype in outs],
        in_specs=[pl.BlockSpec(memory_space=pltpu.VMEM)] * len(args),
        out_specs=[pl.BlockSpec(memory_space=pltpu.VMEM)] * len(outs),
        scratch_shapes=list(scratch),
        compiler_params=pltpu.CompilerParams(vmem_limit_bytes=16 * 2**20),
        cost_estimate=pl.CostEstimate(flops=cost, bytes_accessed=cost, transcendentals=0),
        name=name,
    )(*args)


def dot(left, right, left_dim, right_dim):
    dims = (((left_dim,), (right_dim,)), ((), ()))
    return lax.dot_general(left, right, dims, preferred_element_type=F32)


def line(ref, at):
    start = at // 16 * 16
    return ref[start : start + 16][at - start : at - start + 1]


def pick(ref, ask, parts):
    chosen = ref[0:RBLK]
    for part in range(1, parts):
        chosen = jnp.where(ask == part, ref[part * RBLK : (part + 1) * RBLK], chosen)
    return chosen


def ask_kernel(rows, neighbours, ask):
    index = neighbours[...]
    position = lax.div(index, rows) ^ lax.axis_index("samp")
    block = lax.div(lax.rem(index, rows), RBLK)
    count = lax.axis_size("samp")
    best = [
        jnp.max(jnp.where(position == p, block, 0), axis=0, keepdims=True) for p in range(count)
    ]
    best += [jnp.zeros_like(best[0])] * (ask.shape[0] - count)
    best = jnp.max(jnp.concatenate(best, axis=0), axis=1, keepdims=True)
    ask[...] = jnp.broadcast_to(best.astype(F32), ask.shape).astype(BF16)


def map_kernel(neighbours, weight, plf, noted, out, total, inverse, wide):
    rows = neighbours.shape[0]
    listed = neighbours.shape[1]
    count = lax.axis_size("samp")
    me = lax.axis_index("samp")
    sample = lax.broadcasted_iota(jnp.int32, (RBLK, listed), 0).astype(F32).astype(BF16)
    device = lax.broadcasted_iota(jnp.int32, (count, listed), 0)
    one, zero = jnp.ones((), BF16), jnp.zeros((), BF16)

    def step(i, carry):
        start = pl.multiple_of(i * GROUP, GROUP)
        index = neighbours[pl.ds(start, GROUP), :]
        heavy = weight[pl.ds(start, GROUP), :].astype(F32)
        position = lax.div(index, rows) ^ me
        low = lax.rem(index, RBLK).astype(F32).astype(BF16)
        for r in range(0, GROUP, 2):
            low_one = jnp.concatenate(
                [jnp.where(sample == low[q : q + 1], one, zero) for q in (r, r + 1)], axis=1
            )
            high = [
                jnp.where(device == position[q : q + 1], heavy[q : q + 1], 0.0) for q in (r, r + 1)
            ]
            none = jnp.zeros_like(high[0])
            high_one = jnp.concatenate(
                [jnp.concatenate([high[0], none], axis=1), jnp.concatenate([none, high[1]], axis=1)],
                axis=0,
            ).astype(BF16)
            both = dot(high_one, low_one, 1, 1)
            wide[:, pl.ds(start + r, 1), :] = both[:count].reshape(count, 1, RBLK)
            wide[:, pl.ds(start + r + 1, 1), :] = both[count:].reshape(count, 1, RBLK)
        return carry

    lax.fori_loop(0, rows // GROUP, step, 0, unroll=8)
    for p in range(count):
        out[:, p * RBLK : (p + 1) * RBLK] = wide[p].astype(BF16)
    summed = jnp.sum(weight[...].astype(F32), axis=1, keepdims=True)
    total[...] = jnp.broadcast_to(summed, total.shape)
    inverse[...] = 1.0 / plf[...]


def bin_rows(bins):
    return lax.broadcasted_iota(jnp.int32, (NGC, bins.shape[1]), 0) == bins[...]


def stats_kernel(coverage, bins, stats):
    stats[...] = dot(bin_rows(bins).astype(F32).astype(BF16), coverage[...], 1, 1)


def spread_bins(scale, bins):
    terms = []
    for _ in range(3):
        terms.append(scale.astype(BF16).astype(F32))
        scale = scale - terms[-1]
    picked = bin_rows(bins).astype(F32)
    left = jnp.concatenate(terms, axis=0).astype(BF16)
    return dot(left, jnp.concatenate([picked] * 3, axis=0).astype(BF16), 0, 0)


def norm_kernel(coverage, mine, theirs, bins, ask, noted, plain):
    rows, cols = coverage.shape[0] - LANE, coverage.shape[1]
    extra = ask.shape[0]
    sums = mine[:, 0:rows] + theirs[:, 0:rows]
    number = mine[:, rows : rows + 1] + theirs[:, rows : rows + 1]
    mean = jnp.sum(sums, axis=0, keepdims=True) / (cols * lax.axis_size("tgt"))
    scale = mean / (sums / jnp.maximum(number, 1.0))
    scale = spread_bins(jnp.where(sums > 0, scale, 0.0), bins)
    block = (coverage[0:rows].astype(F32) * scale).astype(BF16)
    plain[0:rows] = block
    noted[0:rows] = block
    noted[rows : rows + extra] = ask[...]


def pass_kernel(late, asked, total, own, across, *refs):
    mates = len(refs) // 2
    half = mates + 1
    order, out = order_of(NOTED, half), refs[mates:]
    rows = own.shape[0] - asked
    parts = rows // RBLK
    for k in range(1, half):
        note = refs[order.index(k)]
        base = note.shape[0] - asked
        other = base + (k ^ block_across(half))
        out[k - 1][0:RBLK] = pick(across, line(note, other), parts)
        if k in late:
            out[k - 1][RBLK : 2 * RBLK] = pick(own, line(note, base + k), parts)


def spread(first, second, third, normf, ratio, rel, own_sum, part):
    inverse = 1.0 / second
    scaled = first * inverse
    ratio[...] = normf * scaled
    relative = (third * inverse) * scaled - 1.0
    rel[...] = relative
    own_sum[...] = jnp.broadcast_to(jnp.sum(relative, axis=1, keepdims=True), own_sum.shape)
    for start in range(0, own_sum.shape[0], LANE):
        block = jnp.where(diagonal(), own_sum[start : start + LANE], 0.0)
        part[:, start : start + LANE] = jnp.sum(block, axis=0, keepdims=True)


def diagonal():
    row = lax.broadcasted_iota(jnp.int32, (LANE, LANE), 0)
    return row == lax.broadcasted_iota(jnp.int32, (LANE, LANE), 1)


def squared(block):
    wide = block.astype(F32)
    return (wide * wide).astype(BF16)


def columns(weight, positions):
    return jnp.concatenate([weight[:, p * RBLK : (p + 1) * RBLK] for p in positions], axis=1)


def place(table, positions):
    return jnp.concatenate([table[p * RBLK : (p + 1) * RBLK] for p in positions], axis=0)


def early_one_kernel(early, rows, weight, own, across, ask, *refs):
    noted, (table, partial) = refs[:-2], refs[-2:]
    parts = rows // RBLK
    half = len(noted) + 1
    for p in early:
        source = own if p == 0 else across if p == early[-1] else noted[p - 1]
        table[p * RBLK : (p + 1) * RBLK] = pick(source, line(ask, p), parts)
    mine, block = columns(weight, early), place(table, early)
    partial[0] = dot(mine, block, 1, 0)
    partial[1] = dot(mine, squared(block), 1, 0)


def first_kernel(late, rows, weight, total, own, early, partial, *refs):
    mates = len(refs) - 5
    half = mates + 1
    order, (table, ratio, rel, own_sum, part) = order_of(PASSED, half), refs[mates:]
    cols = own.shape[1]
    table[...] = early[...]
    arrived = []
    for k, ref in zip(order, refs):
        if k in late:
            arrived.append(k)
            table[k * RBLK : (k + 1) * RBLK] = ref[RBLK : 2 * RBLK]
        other = k ^ block_across(half)
        arrived.append(other)
        table[other * RBLK : (other + 1) * RBLK] = ref[0:RBLK]
    mine, block = columns(weight, arrived), place(table, arrived)
    second = partial[0] + dot(mine, block, 1, 0)
    third = partial[1] + dot(mine, squared(block), 1, 0)
    first = jnp.concatenate([total[...]] * (cols // LANE), axis=1)
    spread(first, second, third, own[0:rows].astype(F32), ratio, rel, own_sum, part)


def gated(weight, table, gates, positions):
    mine, block = columns(weight, positions), place(table, positions)
    wide = gates.astype(F32)
    covs = (wide * block.astype(F32)).astype(BF16)
    squares = (wide * squared(block).astype(F32)).astype(BF16)
    return [dot(mine, values, 1, 0) for values in (gates, covs, squares)]


def early_two_kernel(early, weight, table, gate, across, ask, *refs):
    arrived, partial = refs[:-1], refs[-1]
    parts = gate.shape[0] // RBLK
    far = early[-1]
    gates = [pick(gate, line(ask, 0), parts)] + [ref[...] for ref in arrived]
    gates = jnp.concatenate(gates + [pick(across, line(ask, far), parts)], axis=0)
    for i, moment in enumerate(gated(weight, table, gates, early)):
        partial[i] = moment


def more_two_kernel(positions, weight, table, before, *refs):
    arrived, partial = refs[:-1], refs[-1]
    gates = jnp.concatenate([ref[...] for ref in arrived], axis=0)
    for i, moment in enumerate(gated(weight, table, gates, positions)):
        partial[i] = before[i] + moment


def second_kernel(late, rows, weight, table, own, partial, *refs):
    arrived, (ratio, rel, own_sum, part) = refs[:-4], refs[-4:]
    gates = jnp.concatenate([ref[...] for ref in arrived], axis=0)
    moments = gated(weight, table, gates, late)
    first, second, third = [partial[i] + moment for i, moment in enumerate(moments)]
    spread(first, second, third, own[0:rows].astype(F32), ratio, rel, own_sum, part)


def called(ratio, rel, own_sum, theirs, inverse, finish):
    rows, cols = ratio.shape
    share = 0.5 / (cols * lax.axis_size("tgt"))
    root_half = math.sqrt(0.5 * math.log2(math.e))
    for begin in range(0, rows, LANE):
        row = jnp.broadcast_to(theirs[:, begin : begin + LANE], (LANE, LANE))
        column = jnp.sum(jnp.where(diagonal(), row, 0.0), axis=1, keepdims=True)
        shared = (own_sum[begin : begin + LANE] + column) * share
        for start in range(0, LANE, CHUNK):
            here = slice(begin + start, begin + start + CHUNK)
            spot = shared[start : start + CHUNK]
            by_ploidy = inverse[here]
            step = by_ploidy * root_half
            for lane in range(0, cols, LANE):
                there = slice(lane, lane + LANE)
                level = 0.5 * rel[here, there] + spot
                copies = ratio[here, there] * root_half
                grow = level * by_ploidy
                scores, roots = [], []
                for state, prior in enumerate(LOG_PRIOR):
                    if state == 0:
                        var, delta = 0.25 * level + 0.01, copies - 0.1 * step
                    elif state == 1:
                        var, delta = grow + 0.01, copies - step
                    else:
                        var, delta = var + grow, delta - step
                    roots.append(lax.rsqrt(var))
                    score = delta * roots[state]
                    scores.append(prior * math.log2(math.e) - score * score)
                peak = functools.reduce(jnp.maximum, scores)
                expo = [jnp.exp2(s - peak) * root for s, root in zip(scores, roots)]
                tail = top = expo[5]
                for state in range(4, 0, -1):
                    tail = tail + expo[state]
                    top = top + tail
                finish(here, there, top / (tail + expo[0]))


def gate_kernel(order, asked, ratio, rel, own_sum, theirs, inverse, plf, *refs):
    rows = ratio.shape[0]
    noted, gate, out = refs[: len(order)], refs[len(order)], refs[len(order) + 1 :]

    def finish(here, there, value):
        offset = value - plf[here]
        gate[here, there] = (1.0 / (1.0 + 4.0 * (offset * offset))).astype(BF16)

    called(ratio, rel, own_sum, theirs, inverse, finish)
    for k, ref in zip(order, out):
        spot = noted[k - 1].shape[0] - asked + k
        ref[...] = pick(gate, line(noted[k - 1], spot), rows // RBLK)


def pass_gate_kernel(order, asked, across, *refs):
    noted, out = refs[: len(order)], refs[len(order) :]
    far = gate_across(len(order) + 1)
    for k, ref in zip(order, out):
        spot = noted[k - 1].shape[0] - asked + (k ^ far)
        ref[...] = pick(across, line(noted[k - 1], spot), across.shape[0] // RBLK)


def final_kernel(ratio, rel, own_sum, theirs, inverse, out):
    def finish(here, there, value):
        out[here, there] = value

    called(ratio, rel, own_sum, theirs, inverse, finish)


def body(coverage, neighbours, nbr_weight, ploidy, gc_bin):
    count = lax.axis_size("samp")
    half = count // 2
    mates = range(1, half)
    rows, cols = coverage.shape
    extra = -(-count // 16) * 16
    late = [3] if half > 3 else []
    bins = gc_bin.reshape(1, cols)
    counted = jnp.pad(coverage, ((0, LANE), (0, 0)), constant_values=1)
    plf = jnp.broadcast_to(ploidy.astype(F32)[:, None], (rows, LANE))

    (mine,) = call(stats_kernel, "bin_sums", [((NGC, rows + LANE), F32)], counted, bins)
    theirs = swap_tgt(mine)
    (ask,) = call(
        functools.partial(ask_kernel, rows), "choices", [((extra, cols), BF16)], neighbours
    )
    own, plain = call(
        norm_kernel, "normalise",
        [((rows + extra, cols), BF16), ((rows + SPARE, cols), BF16)],
        counted, mine, theirs, bins, ask,
    )
    across = send(plain, block_across(half), count)
    noted = [send(ask if k in late else own, k, count) for k in mates]
    weight, total, inverse = call(
        map_kernel, "weight_map",
        [((rows, count * RBLK), BF16), ((rows, LANE), F32), ((rows, LANE), F32)],
        neighbours, nbr_weight, plf, own, scratch=[pltpu.VMEM((count, rows, RBLK), F32)],
    )
    passed = call(
        functools.partial(pass_kernel, late, extra), "pass_on",
        [(((2 if k in late else 1) * RBLK, cols), BF16) for k in mates],
        total, own, across, *[noted[k - 1] for k in order_of(NOTED, half)],
    )
    passed = [send(block, k, count) for k, block in zip(mates, passed)]
    spreads = [((rows, cols), F32), ((rows, cols), F32), ((rows, LANE), F32), ((1, rows), F32)]
    early = [0] + [k for k in mates if k not in late] + [block_across(half)]
    table, partial = call(
        functools.partial(early_one_kernel, early, rows), "early_moments_one",
        [((count * RBLK, cols), BF16), ((2, rows, cols), F32)],
        weight, own, across, ask, *noted,
    )
    table, ratio, rel, own_sum, part = call(
        functools.partial(first_kernel, late, rows), "moments_one",
        [((count * RBLK, cols), BF16)] + spreads,
        weight, total, own, table, partial, *[passed[k - 1] for k in order_of(PASSED, half)],
    )
    order = order_of(OWN_GATES, half)
    gate, *gates = call(
        functools.partial(gate_kernel, order, extra), "gate",
        [((rows, cols), BF16)] + [((RBLK, cols), BF16)] * len(order),
        ratio, rel, own_sum, swap_tgt(part), inverse, plf, *noted,
    )
    far = gate_across(half)
    far_gate = send(gate, far, count)
    gates = [send(block, k, count) for k, block in zip(order, gates)]
    (partial,) = call(
        functools.partial(early_two_kernel, [0] + order + [far]), "early_moments_two",
        [((3, rows, cols), F32)], weight, table, gate, far_gate, ask, *gates,
    )
    order = order_of(PASSED_GATES, half)
    gates = call(
        functools.partial(pass_gate_kernel, order, extra), "pass_on_gate",
        [((RBLK, cols), BF16)] * len(order), far_gate, *noted,
    )
    gates = [send(block, k, count) for k, block in zip(order, gates)]
    late = [k ^ far for k in order]
    if len(late) > 1:
        (partial,) = call(
            functools.partial(more_two_kernel, late[:-1]), "more_moments_two",
            [((3, rows, cols), F32)], weight, table, partial, *gates[:-1],
        )
    ratio, rel, own_sum, part = call(
        functools.partial(second_kernel, late[-1:], rows), "moments_two", spreads,
        weight, table, own, partial, gates[-1],
    )
    (out,) = call(
        final_kernel, "copy_number", [((rows, cols), F32)],
        ratio, rel, own_sum, swap_tgt(part), inverse,
    )
    return out


def solution(mesh):
    in_specs = (
        P("samp", ("slab", "tgt")),
        P("samp", None),
        P("samp", None),
        P("samp"),
        P(("slab", "tgt")),
    )
    out_specs = P("samp", ("slab", "tgt"))
    return jax.shard_map(body, mesh=mesh, in_specs=in_specs, out_specs=out_specs, check_vma=False)
```

```python
import functools
import math

import jax
import jax.numpy as jnp
from jax import lax
from jax.experimental import pallas as pl
from jax.experimental.pallas import tpu as pltpu
from jax.sharding import PartitionSpec as P

NGC = 8
RBLK = 128
LANE = 128
CHUNK = 16
GROUP = 16

LOG_PRIOR = (-4.6051702, -3.2188758, -0.1625189, -2.8134107, -3.5065579, -4.6051702)

F32 = jnp.float32
BF16 = jnp.bfloat16


def swap_tgt(value):
    return lax.ppermute(value, "tgt", [(0, 1), (1, 0)])


def send(value, step, count):
    return lax.ppermute(value, "samp", [(i, i ^ step) for i in range(count)])


BLOCK_ACROSS, GATE_ACROSS = 4, 6
NOTED, PASSED, OWN_GATES, PASSED_GATES = (1, 2, 3), (3, 2, 1), (3, 2, 1), (3, 1, 2)
SPARE = 0


def order_of(given, half):
    return list(given) if half == 4 else list(range(1, half))


def block_across(half):
    return BLOCK_ACROSS if half == 4 else half


def gate_across(half):
    return GATE_ACROSS if half == 4 else half


def call(body, name, outs, *args, scratch=(), cost=1):
    return pl.pallas_call(
        body,
        out_shape=[jax.ShapeDtypeStruct(shape, dtype) for shape, dtype in outs],
        in_specs=[pl.BlockSpec(memory_space=pltpu.VMEM)] * len(args),
        out_specs=[pl.BlockSpec(memory_space=pltpu.VMEM)] * len(outs),
        scratch_shapes=list(scratch),
        compiler_params=pltpu.CompilerParams(vmem_limit_bytes=16 * 2**20),
        cost_estimate=pl.CostEstimate(flops=cost, bytes_accessed=cost, transcendentals=0),
        name=name,
    )(*args)


def dot(left, right, left_dim, right_dim):
    dims = (((left_dim,), (right_dim,)), ((), ()))
    return lax.dot_general(left, right, dims, preferred_element_type=F32)


def line(ref, at):
    start = at // 16 * 16
    return ref[start : start + 16][at - start : at - start + 1]


def pick(ref, ask, parts):
    chosen = ref[0:RBLK]
    for part in range(1, parts):
        chosen = jnp.where(ask == part, ref[part * RBLK : (part + 1) * RBLK], chosen)
    return chosen


def ask_kernel(rows, neighbours, ask):
    index = neighbours[...]
    position = lax.div(index, rows) ^ lax.axis_index("samp")
    block = lax.div(lax.rem(index, rows), RBLK)
    count = lax.axis_size("samp")
    best = [
        jnp.max(jnp.where(position == p, block, 0), axis=0, keepdims=True) for p in range(count)
    ]
    best += [jnp.zeros_like(best[0])] * (ask.shape[0] - count)
    best = jnp.max(jnp.concatenate(best, axis=0), axis=1, keepdims=True)
    ask[...] = jnp.broadcast_to(best.astype(F32), ask.shape).astype(BF16)


def map_kernel(neighbours, weight, plf, noted, out, total, inverse, wide):
    rows = neighbours.shape[0]
    listed = neighbours.shape[1]
    count = lax.axis_size("samp")
    me = lax.axis_index("samp")
    sample = lax.broadcasted_iota(jnp.int32, (RBLK, listed), 0).astype(F32).astype(BF16)
    device = lax.broadcasted_iota(jnp.int32, (count, listed), 0)
    one, zero = jnp.ones((), BF16), jnp.zeros((), BF16)

    def step(i, carry):
        start = pl.multiple_of(i * GROUP, GROUP)
        index = neighbours[pl.ds(start, GROUP), :]
        heavy = weight[pl.ds(start, GROUP), :].astype(F32)
        position = lax.div(index, rows) ^ me
        low = lax.rem(index, RBLK).astype(F32).astype(BF16)
        for r in range(0, GROUP, 2):
            low_one = jnp.concatenate(
                [jnp.where(sample == low[q : q + 1], one, zero) for q in (r, r + 1)], axis=1
            )
            high = [
                jnp.where(device == position[q : q + 1], heavy[q : q + 1], 0.0) for q in (r, r + 1)
            ]
            none = jnp.zeros_like(high[0])
            high_one = jnp.concatenate(
                [jnp.concatenate([high[0], none], axis=1), jnp.concatenate([none, high[1]], axis=1)],
                axis=0,
            ).astype(BF16)
            both = dot(high_one, low_one, 1, 1)
            wide[:, pl.ds(start + r, 1), :] = both[:count].reshape(count, 1, RBLK)
            wide[:, pl.ds(start + r + 1, 1), :] = both[count:].reshape(count, 1, RBLK)
        return carry

    lax.fori_loop(0, rows // GROUP, step, 0, unroll=8)
    for p in range(count):
        out[:, p * RBLK : (p + 1) * RBLK] = wide[p].astype(BF16)
    summed = jnp.sum(weight[...].astype(F32), axis=1, keepdims=True)
    total[...] = jnp.broadcast_to(summed, total.shape)
    inverse[...] = 1.0 / plf[...]


def bin_rows(bins):
    return lax.broadcasted_iota(jnp.int32, (NGC, bins.shape[1]), 0) == bins[...]


def stats_kernel(coverage, bins, stats):
    stats[...] = dot(bin_rows(bins).astype(F32).astype(BF16), coverage[...], 1, 1)


def spread_bins(scale, bins):
    terms = []
    for _ in range(3):
        terms.append(scale.astype(BF16).astype(F32))
        scale = scale - terms[-1]
    picked = bin_rows(bins).astype(F32)
    left = jnp.concatenate(terms, axis=0).astype(BF16)
    return dot(left, jnp.concatenate([picked] * 3, axis=0).astype(BF16), 0, 0)


def norm_kernel(coverage, mine, theirs, bins, ask, noted, plain):
    rows, cols = coverage.shape[0] - LANE, coverage.shape[1]
    extra = ask.shape[0]
    sums = mine[:, 0:rows] + theirs[:, 0:rows]
    number = mine[:, rows : rows + 1] + theirs[:, rows : rows + 1]
    mean = jnp.sum(sums, axis=0, keepdims=True) / (cols * lax.axis_size("tgt"))
    scale = mean / (sums / jnp.maximum(number, 1.0))
    scale = spread_bins(jnp.where(sums > 0, scale, 0.0), bins)
    block = (coverage[0:rows].astype(F32) * scale).astype(BF16)
    plain[0:rows] = block
    noted[0:rows] = block
    noted[rows : rows + extra] = ask[...]


def pass_kernel(late, asked, total, own, across, *refs):
    mates = len(refs) // 2
    half = mates + 1
    order, out = order_of(NOTED, half), refs[mates:]
    rows = own.shape[0] - asked
    parts = rows // RBLK
    for k in range(1, half):
        note = refs[order.index(k)]
        base = note.shape[0] - asked
        other = base + (k ^ block_across(half))
        out[k - 1][0:RBLK] = pick(across, line(note, other), parts)
        if k in late:
            out[k - 1][RBLK : 2 * RBLK] = pick(own, line(note, base + k), parts)


def spread(first, second, third, normf, ratio, rel, own_sum, part):
    inverse = 1.0 / second
    scaled = first * inverse
    ratio[...] = normf * scaled
    relative = (third * inverse) * scaled - 1.0
    rel[...] = relative
    own_sum[...] = jnp.broadcast_to(jnp.sum(relative, axis=1, keepdims=True), own_sum.shape)
    for start in range(0, own_sum.shape[0], LANE):
        block = jnp.where(diagonal(), own_sum[start : start + LANE], 0.0)
        part[:, start : start + LANE] = jnp.sum(block, axis=0, keepdims=True)


def diagonal():
    row = lax.broadcasted_iota(jnp.int32, (LANE, LANE), 0)
    return row == lax.broadcasted_iota(jnp.int32, (LANE, LANE), 1)


def squared(block):
    wide = block.astype(F32)
    return (wide * wide).astype(BF16)


def columns(weight, positions):
    return jnp.concatenate([weight[:, p * RBLK : (p + 1) * RBLK] for p in positions], axis=1)


def place(table, positions):
    return jnp.concatenate([table[p * RBLK : (p + 1) * RBLK] for p in positions], axis=0)


def early_one_kernel(early, rows, weight, own, across, ask, *refs):
    noted, (table, partial) = refs[:-2], refs[-2:]
    parts = rows // RBLK
    half = len(noted) + 1
    for p in early:
        source = own if p == 0 else across if p == early[-1] else noted[p - 1]
        table[p * RBLK : (p + 1) * RBLK] = pick(source, line(ask, p), parts)
    mine, block = columns(weight, early), place(table, early)
    partial[0] = dot(mine, block, 1, 0)
    partial[1] = dot(mine, squared(block), 1, 0)


def arrivals(late, order, half, refs):
    found = []
    for k, ref in zip(order, refs):
        if k in late:
            found.append((k, ref[RBLK : 2 * RBLK]))
        found.append((k ^ block_across(half), ref[0:RBLK]))
    return zip(*found)


def add_kernel(late, order, half, weight, early, before, *refs):
    passed, (table, partial) = refs[:-2], refs[-2:]
    positions, blocks = arrivals(late, order, half, passed)
    table[...] = early[...]
    for p, block in zip(positions, blocks):
        table[p * RBLK : (p + 1) * RBLK] = block
    mine, block = columns(weight, positions), jnp.concatenate(blocks, axis=0)
    partial[0] = before[0] + dot(mine, block, 1, 0)
    partial[1] = before[1] + dot(mine, squared(block), 1, 0)


def first_kernel(late, order, half, rows, weight, total, own, before, passed, *refs):
    positions, blocks = arrivals(late, order, half, [passed])
    mine, block = columns(weight, positions), jnp.concatenate(blocks, axis=0)
    second = before[0] + dot(mine, block, 1, 0)
    third = before[1] + dot(mine, squared(block), 1, 0)
    first = jnp.concatenate([total[...]] * (own.shape[1] // LANE), axis=1)
    spread(first, second, third, own[0:rows].astype(F32), *refs)


def fill_kernel(late, order, half, early, passed, ratio, table):
    positions, blocks = arrivals(late, order, half, [passed])
    table[...] = early[...]
    for p, block in zip(positions, blocks):
        table[p * RBLK : (p + 1) * RBLK] = block


def gated(weight, table, gates, positions):
    mine, block = columns(weight, positions), place(table, positions)
    wide = gates.astype(F32)
    covs = (wide * block.astype(F32)).astype(BF16)
    squares = (wide * squared(block).astype(F32)).astype(BF16)
    return [dot(mine, values, 1, 0) for values in (gates, covs, squares)]


def early_two_kernel(early, weight, table, gate, across, ask, *refs):
    arrived, partial = refs[:-1], refs[-1]
    parts = gate.shape[0] // RBLK
    far = early[-1]
    gates = [pick(gate, line(ask, 0), parts)] + [ref[...] for ref in arrived]
    gates = jnp.concatenate(gates + [pick(across, line(ask, far), parts)], axis=0)
    for i, moment in enumerate(gated(weight, table, gates, early)):
        partial[i] = moment


def more_two_kernel(positions, weight, table, before, *refs):
    arrived, partial = refs[:-1], refs[-1]
    gates = jnp.concatenate([ref[...] for ref in arrived], axis=0)
    for i, moment in enumerate(gated(weight, table, gates, positions)):
        partial[i] = before[i] + moment


def second_kernel(late, rows, weight, table, own, partial, *refs):
    arrived, (ratio, rel, own_sum, part) = refs[:-4], refs[-4:]
    gates = jnp.concatenate([ref[...] for ref in arrived], axis=0)
    moments = gated(weight, table, gates, late)
    first, second, third = [partial[i] + moment for i, moment in enumerate(moments)]
    spread(first, second, third, own[0:rows].astype(F32), ratio, rel, own_sum, part)


def called(ratio, rel, own_sum, theirs, inverse, finish):
    rows, cols = ratio.shape
    share = 0.5 / (cols * lax.axis_size("tgt"))
    root_half = math.sqrt(0.5 * math.log2(math.e))
    for begin in range(0, rows, LANE):
        row = jnp.broadcast_to(theirs[:, begin : begin + LANE], (LANE, LANE))
        column = jnp.sum(jnp.where(diagonal(), row, 0.0), axis=1, keepdims=True)
        shared = (own_sum[begin : begin + LANE] + column) * share
        for start in range(0, LANE, CHUNK):
            here = slice(begin + start, begin + start + CHUNK)
            spot = shared[start : start + CHUNK]
            by_ploidy = inverse[here]
            step = by_ploidy * root_half
            for lane in range(0, cols, LANE):
                there = slice(lane, lane + LANE)
                level = 0.5 * rel[here, there] + spot
                copies = ratio[here, there] * root_half
                grow = level * by_ploidy
                scores, roots = [], []
                for state, prior in enumerate(LOG_PRIOR):
                    if state == 0:
                        var, delta = 0.25 * level + 0.01, copies - 0.1 * step
                    elif state == 1:
                        var, delta = grow + 0.01, copies - step
                    else:
                        var, delta = var + grow, delta - step
                    roots.append(lax.rsqrt(var))
                    score = delta * roots[state]
                    scores.append(prior * math.log2(math.e) - score * score)
                peak = functools.reduce(jnp.maximum, scores)
                expo = [jnp.exp2(s - peak) * root for s, root in zip(scores, roots)]
                tail = top = expo[5]
                for state in range(4, 0, -1):
                    tail = tail + expo[state]
                    top = top + tail
                finish(here, there, top / (tail + expo[0]))


def gate_kernel(order, asked, ratio, rel, own_sum, theirs, inverse, plf, *refs):
    rows = ratio.shape[0]
    noted, gate, out = refs[: len(order)], refs[len(order)], refs[len(order) + 1 :]

    def finish(here, there, value):
        offset = value - plf[here]
        gate[here, there] = (1.0 / (1.0 + 4.0 * (offset * offset))).astype(BF16)

    called(ratio, rel, own_sum, theirs, inverse, finish)
    for k, ref in zip(order, out):
        spot = noted[k - 1].shape[0] - asked + k
        ref[...] = pick(gate, line(noted[k - 1], spot), rows // RBLK)


def pass_gate_kernel(order, asked, across, *refs):
    noted, out = refs[: len(order)], refs[len(order) :]
    far = gate_across(len(order) + 1)
    for k, ref in zip(order, out):
        spot = noted[k - 1].shape[0] - asked + (k ^ far)
        ref[...] = pick(across, line(noted[k - 1], spot), across.shape[0] // RBLK)


def final_kernel(ratio, rel, own_sum, theirs, inverse, out):
    def finish(here, there, value):
        out[here, there] = value

    called(ratio, rel, own_sum, theirs, inverse, finish)


def body(coverage, neighbours, nbr_weight, ploidy, gc_bin):
    count = lax.axis_size("samp")
    half = count // 2
    mates = range(1, half)
    rows, cols = coverage.shape
    extra = -(-count // 16) * 16
    late = [3] if half > 3 else []
    bins = gc_bin.reshape(1, cols)
    counted = jnp.pad(coverage, ((0, LANE), (0, 0)), constant_values=1)
    plf = jnp.broadcast_to(ploidy.astype(F32)[:, None], (rows, LANE))

    (mine,) = call(stats_kernel, "bin_sums", [((NGC, rows + LANE), F32)], counted, bins)
    theirs = swap_tgt(mine)
    (ask,) = call(
        functools.partial(ask_kernel, rows), "choices", [((extra, cols), BF16)], neighbours
    )
    own, plain = call(
        norm_kernel, "normalise",
        [((rows + extra, cols), BF16), ((rows + SPARE, cols), BF16)],
        counted, mine, theirs, bins, ask,
    )
    across = send(plain, block_across(half), count)
    noted = [send(ask if k in late else own, k, count) for k in mates]
    weight, total, inverse = call(
        map_kernel, "weight_map",
        [((rows, count * RBLK), BF16), ((rows, LANE), F32), ((rows, LANE), F32)],
        neighbours, nbr_weight, plf, own, scratch=[pltpu.VMEM((count, rows, RBLK), F32)],
    )
    passed = call(
        functools.partial(pass_kernel, late, extra), "pass_on",
        [(((2 if k in late else 1) * RBLK, cols), BF16) for k in mates],
        total, own, across, *[noted[k - 1] for k in order_of(NOTED, half)],
    )
    passed = [send(block, k, count) for k, block in zip(mates, passed)]
    spreads = [((rows, cols), F32), ((rows, cols), F32), ((rows, LANE), F32), ((1, rows), F32)]
    early = [0] + [k for k in mates if k not in late] + [block_across(half)]
    table, partial = call(
        functools.partial(early_one_kernel, early, rows), "early_moments_one",
        [((count * RBLK, cols), BF16), ((2, rows, cols), F32)],
        weight, own, across, ask, *noted,
    )
    order = order_of(PASSED, half)
    passed = [passed[k - 1] for k in order]
    if len(order) > 1:
        table, partial = call(
            functools.partial(add_kernel, late, order[:-1], half), "more_moments_one",
            [((count * RBLK, cols), BF16), ((2, rows, cols), F32)],
            weight, table, partial, *passed[:-1],
        )
    ratio, rel, own_sum, part = call(
        functools.partial(first_kernel, late, order[-1:], half, rows), "moments_one", spreads,
        weight, total, own, partial, passed[-1],
    )
    (table,) = call(
        functools.partial(fill_kernel, late, order[-1:], half), "fill_table",
        [((count * RBLK, cols), BF16)], table, passed[-1], own_sum,
    )
    order = order_of(OWN_GATES, half)
    gate, *gates = call(
        functools.partial(gate_kernel, order, extra), "gate",
        [((rows, cols), BF16)] + [((RBLK, cols), BF16)] * len(order),
        ratio, rel, own_sum, swap_tgt(part), inverse, plf, *noted,
    )
    far = gate_across(half)
    far_gate = send(gate, far, count)
    gates = [send(block, k, count) for k, block in zip(order, gates)]
    (partial,) = call(
        functools.partial(early_two_kernel, [0] + order + [far]), "early_moments_two",
        [((3, rows, cols), F32)], weight, table, gate, far_gate, ask, *gates,
    )
    order = order_of(PASSED_GATES, half)
    gates = call(
        functools.partial(pass_gate_kernel, order, extra), "pass_on_gate",
        [((RBLK, cols), BF16)] * len(order), far_gate, *noted,
    )
    gates = [send(block, k, count) for k, block in zip(order, gates)]
    late = [k ^ far for k in order]
    if len(late) > 1:
        (partial,) = call(
            functools.partial(more_two_kernel, late[:-1]), "more_moments_two",
            [((3, rows, cols), F32)], weight, table, partial, *gates[:-1],
        )
    ratio, rel, own_sum, part = call(
        functools.partial(second_kernel, late[-1:], rows), "moments_two", spreads,
        weight, table, own, partial, gates[-1],
    )
    (out,) = call(
        final_kernel, "copy_number", [((rows, cols), F32)],
        ratio, rel, own_sum, swap_tgt(part), inverse,
    )
    return out


def solution(mesh):
    in_specs = (
        P("samp", ("slab", "tgt")),
        P("samp", None),
        P("samp", None),
        P("samp"),
        P(("slab", "tgt")),
    )
    out_specs = P("samp", ("slab", "tgt"))
    return jax.shard_map(body, mesh=mesh, in_specs=in_specs, out_specs=out_specs, check_vma=False)
```

```python
import functools
import math

import jax
import jax.numpy as jnp
from jax import lax
from jax.experimental import pallas as pl
from jax.experimental.pallas import tpu as pltpu
from jax.sharding import PartitionSpec as P

NGC = 8
RBLK = 128
LANE = 128
CHUNK = 16
GROUP = 16

LOG_PRIOR = (-4.6051702, -3.2188758, -0.1625189, -2.8134107, -3.5065579, -4.6051702)

F32 = jnp.float32
BF16 = jnp.bfloat16


def swap_tgt(value):
    return lax.ppermute(value, "tgt", [(0, 1), (1, 0)])


def send(value, step, count):
    return lax.ppermute(value, "samp", [(i, i ^ step) for i in range(count)])


BLOCK_ACROSS, GATE_ACROSS = 4, 6
NOTED, PASSED, OWN_GATES, PASSED_GATES = (1, 2, 3), (3, 2, 1), (3, 2, 1), (3, 1, 2)
SPARE = 0


def order_of(given, half):
    return list(given) if half == 4 else list(range(1, half))


def block_across(half):
    return BLOCK_ACROSS if half == 4 else half


def gate_across(half):
    return GATE_ACROSS if half == 4 else half


def call(body, name, outs, *args, scratch=(), cost=1):
    return pl.pallas_call(
        body,
        out_shape=[jax.ShapeDtypeStruct(shape, dtype) for shape, dtype in outs],
        in_specs=[pl.BlockSpec(memory_space=pltpu.VMEM)] * len(args),
        out_specs=[pl.BlockSpec(memory_space=pltpu.VMEM)] * len(outs),
        scratch_shapes=list(scratch),
        compiler_params=pltpu.CompilerParams(vmem_limit_bytes=16 * 2**20),
        cost_estimate=pl.CostEstimate(flops=cost, bytes_accessed=cost, transcendentals=0),
        name=name,
    )(*args)


def dot(left, right, left_dim, right_dim):
    dims = (((left_dim,), (right_dim,)), ((), ()))
    return lax.dot_general(left, right, dims, preferred_element_type=F32)


def line(ref, at):
    start = at // 16 * 16
    return ref[start : start + 16][at - start : at - start + 1]


def pick(ref, ask, parts):
    chosen = ref[0:RBLK]
    for part in range(1, parts):
        chosen = jnp.where(ask == part, ref[part * RBLK : (part + 1) * RBLK], chosen)
    return chosen


def ask_kernel(rows, neighbours, ask):
    index = neighbours[...]
    position = lax.div(index, rows) ^ lax.axis_index("samp")
    block = lax.div(lax.rem(index, rows), RBLK)
    count = lax.axis_size("samp")
    best = [
        jnp.max(jnp.where(position == p, block, 0), axis=0, keepdims=True) for p in range(count)
    ]
    best += [jnp.zeros_like(best[0])] * (ask.shape[0] - count)
    best = jnp.max(jnp.concatenate(best, axis=0), axis=1, keepdims=True)
    ask[...] = jnp.broadcast_to(best.astype(F32), ask.shape).astype(BF16)


def map_kernel(neighbours, weight, plf, noted, out, total, inverse, wide):
    rows = neighbours.shape[0]
    listed = neighbours.shape[1]
    count = lax.axis_size("samp")
    me = lax.axis_index("samp")
    sample = lax.broadcasted_iota(jnp.int32, (RBLK, listed), 0).astype(F32).astype(BF16)
    device = lax.broadcasted_iota(jnp.int32, (count, listed), 0)
    one, zero = jnp.ones((), BF16), jnp.zeros((), BF16)

    def step(i, carry):
        start = pl.multiple_of(i * GROUP, GROUP)
        index = neighbours[pl.ds(start, GROUP), :]
        heavy = weight[pl.ds(start, GROUP), :].astype(F32)
        position = lax.div(index, rows) ^ me
        low = lax.rem(index, RBLK).astype(F32).astype(BF16)
        for r in range(0, GROUP, 2):
            low_one = jnp.concatenate(
                [jnp.where(sample == low[q : q + 1], one, zero) for q in (r, r + 1)], axis=1
            )
            high = [
                jnp.where(device == position[q : q + 1], heavy[q : q + 1], 0.0) for q in (r, r + 1)
            ]
            none = jnp.zeros_like(high[0])
            high_one = jnp.concatenate(
                [jnp.concatenate([high[0], none], axis=1), jnp.concatenate([none, high[1]], axis=1)],
                axis=0,
            ).astype(BF16)
            both = dot(high_one, low_one, 1, 1)
            wide[:, pl.ds(start + r, 1), :] = both[:count].reshape(count, 1, RBLK)
            wide[:, pl.ds(start + r + 1, 1), :] = both[count:].reshape(count, 1, RBLK)
        return carry

    lax.fori_loop(0, rows // GROUP, step, 0, unroll=8)
    for p in range(count):
        out[:, p * RBLK : (p + 1) * RBLK] = wide[p].astype(BF16)
    summed = jnp.sum(weight[...].astype(F32), axis=1, keepdims=True)
    total[...] = jnp.broadcast_to(summed, total.shape)
    inverse[...] = 1.0 / plf[...]


def bin_rows(bins):
    return lax.broadcasted_iota(jnp.int32, (NGC, bins.shape[1]), 0) == bins[...]


def stats_kernel(coverage, bins, stats):
    stats[...] = dot(bin_rows(bins).astype(F32).astype(BF16), coverage[...], 1, 1)


def spread_bins(scale, bins):
    terms = []
    for _ in range(3):
        terms.append(scale.astype(BF16).astype(F32))
        scale = scale - terms[-1]
    picked = bin_rows(bins).astype(F32)
    left = jnp.concatenate(terms, axis=0).astype(BF16)
    return dot(left, jnp.concatenate([picked] * 3, axis=0).astype(BF16), 0, 0)


def norm_kernel(coverage, mine, theirs, bins, ask, noted, plain):
    rows, cols = coverage.shape[0] - LANE, coverage.shape[1]
    extra = ask.shape[0]
    sums = mine[:, 0:rows] + theirs[:, 0:rows]
    number = mine[:, rows : rows + 1] + theirs[:, rows : rows + 1]
    mean = jnp.sum(sums, axis=0, keepdims=True) / (cols * lax.axis_size("tgt"))
    scale = mean / (sums / jnp.maximum(number, 1.0))
    scale = spread_bins(jnp.where(sums > 0, scale, 0.0), bins)
    block = (coverage[0:rows].astype(F32) * scale).astype(BF16)
    plain[0:rows] = block
    noted[0:rows] = block
    noted[rows : rows + extra] = ask[...]


def pass_kernel(late, asked, total, own, across, *refs):
    mates = len(refs) // 2
    half = mates + 1
    order, out = order_of(NOTED, half), refs[mates:]
    rows = own.shape[0] - asked
    parts = rows // RBLK
    for k in range(1, half):
        note = refs[order.index(k)]
        base = note.shape[0] - asked
        other = base + (k ^ block_across(half))
        out[k - 1][0:RBLK] = pick(across, line(note, other), parts)
        if k in late:
            out[k - 1][RBLK : 2 * RBLK] = pick(own, line(note, base + k), parts)


def spread(first, second, third, normf, ratio, rel, own_sum, part):
    inverse = 1.0 / second
    scaled = first * inverse
    ratio[...] = normf * scaled
    relative = (third * inverse) * scaled - 1.0
    rel[...] = relative
    own_sum[...] = jnp.broadcast_to(jnp.sum(relative, axis=1, keepdims=True), own_sum.shape)
    for start in range(0, own_sum.shape[0], LANE):
        block = jnp.where(diagonal(), own_sum[start : start + LANE], 0.0)
        part[:, start : start + LANE] = jnp.sum(block, axis=0, keepdims=True)


def diagonal():
    row = lax.broadcasted_iota(jnp.int32, (LANE, LANE), 0)
    return row == lax.broadcasted_iota(jnp.int32, (LANE, LANE), 1)


def squared(block):
    wide = block.astype(F32)
    return (wide * wide).astype(BF16)


def columns(weight, positions):
    return jnp.concatenate([weight[:, p * RBLK : (p + 1) * RBLK] for p in positions], axis=1)


def place(table, positions):
    return jnp.concatenate([table[p * RBLK : (p + 1) * RBLK] for p in positions], axis=0)


def early_one_kernel(early, rows, weight, own, across, ask, *refs):
    noted, (table, partial) = refs[:-2], refs[-2:]
    parts = rows // RBLK
    half = len(noted) + 1
    for p in early:
        source = own if p == 0 else across if p == early[-1] else noted[p - 1]
        table[p * RBLK : (p + 1) * RBLK] = pick(source, line(ask, p), parts)
    mine, block = columns(weight, early), place(table, early)
    partial[0] = dot(mine, block, 1, 0)
    partial[1] = dot(mine, squared(block), 1, 0)


def first_kernel(late, rows, weight, total, own, early, partial, *refs):
    mates = len(refs) - 5
    half = mates + 1
    order, (table, ratio, rel, own_sum, part) = order_of(PASSED, half), refs[mates:]
    cols = own.shape[1]
    table[...] = early[...]
    arrived = []
    for k, ref in zip(order, refs):
        if k in late:
            arrived.append(k)
            table[k * RBLK : (k + 1) * RBLK] = ref[RBLK : 2 * RBLK]
        other = k ^ block_across(half)
        arrived.append(other)
        table[other * RBLK : (other + 1) * RBLK] = ref[0:RBLK]
    mine, block = columns(weight, arrived), place(table, arrived)
    second = partial[0] + dot(mine, block, 1, 0)
    third = partial[1] + dot(mine, squared(block), 1, 0)
    first = jnp.concatenate([total[...]] * (cols // LANE), axis=1)
    spread(first, second, third, own[0:rows].astype(F32), ratio, rel, own_sum, part)


def gated(weight, table, gates, positions):
    mine, block = columns(weight, positions), place(table, positions)
    wide = gates.astype(F32)
    covs = (wide * block.astype(F32)).astype(BF16)
    squares = (wide * squared(block).astype(F32)).astype(BF16)
    return [dot(mine, values, 1, 0) for values in (gates, covs, squares)]


def early_two_kernel(early, weight, table, gate, across, ask, *refs):
    arrived, partial = refs[:-1], refs[-1]
    parts = gate.shape[0] // RBLK
    far = early[-1]
    gates = [pick(gate, line(ask, 0), parts)] + [ref[...] for ref in arrived]
    gates = jnp.concatenate(gates + [pick(across, line(ask, far), parts)], axis=0)
    for i, moment in enumerate(gated(weight, table, gates, early)):
        partial[i] = moment


def second_kernel(late, rows, weight, table, own, partial, *refs):
    arrived, (ratio, rel, own_sum, part) = refs[:-4], refs[-4:]
    gates = jnp.concatenate([ref[...] for ref in arrived], axis=0)
    moments = gated(weight, table, gates, late)
    first, second, third = [partial[i] + moment for i, moment in enumerate(moments)]
    spread(first, second, third, own[0:rows].astype(F32), ratio, rel, own_sum, part)


def called(ratio, rel, own_sum, theirs, inverse, finish):
    rows, cols = ratio.shape
    share = 0.5 / (cols * lax.axis_size("tgt"))
    root_half = math.sqrt(0.5 * math.log2(math.e))
    for begin in range(0, rows, LANE):
        row = jnp.broadcast_to(theirs[:, begin : begin + LANE], (LANE, LANE))
        column = jnp.sum(jnp.where(diagonal(), row, 0.0), axis=1, keepdims=True)
        shared = (own_sum[begin : begin + LANE] + column) * share
        for start in range(0, LANE, CHUNK):
            here = slice(begin + start, begin + start + CHUNK)
            spot = shared[start : start + CHUNK]
            by_ploidy = inverse[here]
            step = by_ploidy * root_half
            for lane in range(0, cols, LANE):
                there = slice(lane, lane + LANE)
                level = 0.5 * rel[here, there] + spot
                copies = ratio[here, there] * root_half
                grow = level * by_ploidy
                scores, roots = [], []
                for state, prior in enumerate(LOG_PRIOR):
                    if state == 0:
                        var, delta = 0.25 * level + 0.01, copies - 0.1 * step
                    elif state == 1:
                        var, delta = grow + 0.01, copies - step
                    else:
                        var, delta = var + grow, delta - step
                    roots.append(lax.rsqrt(var))
                    score = delta * roots[state]
                    scores.append(prior * math.log2(math.e) - score * score)
                peak = functools.reduce(jnp.maximum, scores)
                expo = [jnp.exp2(s - peak) * root for s, root in zip(scores, roots)]
                tail = top = expo[5]
                for state in range(4, 0, -1):
                    tail = tail + expo[state]
                    top = top + tail
                finish(here, there, top / (tail + expo[0]))


def gate_kernel(ratio, rel, own_sum, theirs, inverse, plf, gate):
    def finish(here, there, value):
        offset = value - plf[here]
        gate[here, there] = (1.0 / (1.0 + 4.0 * (offset * offset))).astype(BF16)

    called(ratio, rel, own_sum, theirs, inverse, finish)


def own_gate_kernel(order, asked, gate, *refs):
    noted, out = refs[: len(order)], refs[len(order) :]
    for k, ref in zip(order, out):
        spot = noted[k - 1].shape[0] - asked + k
        ref[...] = pick(gate, line(noted[k - 1], spot), gate.shape[0] // RBLK)


def pass_gate_kernel(order, asked, across, *refs):
    noted, out = refs[: len(order)], refs[len(order) :]
    far = gate_across(len(order) + 1)
    for k, ref in zip(order, out):
        spot = noted[k - 1].shape[0] - asked + (k ^ far)
        ref[...] = pick(across, line(noted[k - 1], spot), across.shape[0] // RBLK)


def final_kernel(ratio, rel, own_sum, theirs, inverse, out):
    def finish(here, there, value):
        out[here, there] = value

    called(ratio, rel, own_sum, theirs, inverse, finish)


def body(coverage, neighbours, nbr_weight, ploidy, gc_bin):
    count = lax.axis_size("samp")
    half = count // 2
    mates = range(1, half)
    rows, cols = coverage.shape
    extra = -(-count // 16) * 16
    late = [3] if half > 3 else []
    bins = gc_bin.reshape(1, cols)
    counted = jnp.pad(coverage, ((0, LANE), (0, 0)), constant_values=1)
    plf = jnp.broadcast_to(ploidy.astype(F32)[:, None], (rows, LANE))

    (mine,) = call(stats_kernel, "bin_sums", [((NGC, rows + LANE), F32)], counted, bins)
    theirs = swap_tgt(mine)
    (ask,) = call(
        functools.partial(ask_kernel, rows), "choices", [((extra, cols), BF16)], neighbours
    )
    own, plain = call(
        norm_kernel, "normalise",
        [((rows + extra, cols), BF16), ((rows + SPARE, cols), BF16)],
        counted, mine, theirs, bins, ask,
    )
    across = send(plain, block_across(half), count)
    noted = [send(ask if k in late else own, k, count) for k in mates]
    weight, total, inverse = call(
        map_kernel, "weight_map",
        [((rows, count * RBLK), BF16), ((rows, LANE), F32), ((rows, LANE), F32)],
        neighbours, nbr_weight, plf, own, scratch=[pltpu.VMEM((count, rows, RBLK), F32)],
    )
    passed = call(
        functools.partial(pass_kernel, late, extra), "pass_on",
        [(((2 if k in late else 1) * RBLK, cols), BF16) for k in mates],
        total, own, across, *[noted[k - 1] for k in order_of(NOTED, half)],
    )
    passed = [send(block, k, count) for k, block in zip(mates, passed)]
    spreads = [((rows, cols), F32), ((rows, cols), F32), ((rows, LANE), F32), ((1, rows), F32)]
    early = [0] + [k for k in mates if k not in late] + [block_across(half)]
    table, partial = call(
        functools.partial(early_one_kernel, early, rows), "early_moments_one",
        [((count * RBLK, cols), BF16), ((2, rows, cols), F32)],
        weight, own, across, ask, *noted,
    )
    table, ratio, rel, own_sum, part = call(
        functools.partial(first_kernel, late, rows), "moments_one",
        [((count * RBLK, cols), BF16)] + spreads,
        weight, total, own, table, partial, *[passed[k - 1] for k in order_of(PASSED, half)],
    )
    order = order_of(OWN_GATES, half)
    (gate,) = call(
        gate_kernel, "gate", [((rows, cols), BF16)],
        ratio, rel, own_sum, swap_tgt(part), inverse, plf,
    )
    gates = call(
        functools.partial(own_gate_kernel, order, extra), "own_gates",
        [((RBLK, cols), BF16)] * len(order), gate, *noted,
    )
    far = gate_across(half)
    far_gate = send(gate, far, count)
    gates = [send(block, k, count) for k, block in zip(order, gates)]
    (partial,) = call(
        functools.partial(early_two_kernel, [0] + order + [far]), "early_moments_two",
        [((3, rows, cols), F32)], weight, table, gate, far_gate, ask, *gates,
    )
    order = order_of(PASSED_GATES, half)
    gates = call(
        functools.partial(pass_gate_kernel, order, extra), "pass_on_gate",
        [((RBLK, cols), BF16)] * len(order), far_gate, *noted,
    )
    gates = [send(block, k, count) for k, block in zip(order, gates)]
    ratio, rel, own_sum, part = call(
        functools.partial(second_kernel, [k ^ far for k in order], rows), "moments_two", spreads,
        weight, table, own, partial, *gates,
    )
    (out,) = call(
        final_kernel, "copy_number", [((rows, cols), F32)],
        ratio, rel, own_sum, swap_tgt(part), inverse,
    )
    return out


def solution(mesh):
    in_specs = (
        P("samp", ("slab", "tgt")),
        P("samp", None),
        P("samp", None),
        P("samp"),
        P(("slab", "tgt")),
    )
    out_specs = P("samp", ("slab", "tgt"))
    return jax.shard_map(body, mesh=mesh, in_specs=in_specs, out_specs=out_specs, check_vma=False)
```
